32 devices in a mesh: groups: 2 (over x), seq: 8 (over z, y), head: 2 (over core).
Axes of the slice: x: 2, y: 2, z: 4, core: 2. Of those that a mesh axis runs over, the one named last changes fastest.
Arguments:
- kv: bfloat16 [32, 4096, 576], P(('groups', 'seq'), 'head'), parts along dimension 0, as said below
- lengths: int32 [32], P('groups'), parts along dimension 0, may hold values from 512 to 4096, as said below
- slot_of: int32 [32], P('groups'), parts along dimension 0, may hold values from 0 to 15, as said below
- query: bfloat16 [4, 32, 128, 576], P(None, ('groups', 'seq'), 'head'), parts along dimension 1
- new_latent: bfloat16 [4, 32, 576], P(None, ('groups', 'seq')), parts along dimension 1, may hold values from -6 to 6
Outputs:
- attended: bfloat16 [4, 32, 128, 512], P(None, ('groups', 'seq'), 'head'), parts along dimension 1
- owned_cache: bfloat16 [32, 4096, 576], P(('groups', 'seq'), 'head'), parts along dimension 0
The draws below stay inside these ranges and needn't reach their ends.
There are 2 independent parts, one for each index of `groups`. The reference program is written for one: setup_inputs(seed, part) draws one part's arguments, and reference() takes and returns one part's arrays. A program takes and returns all parts, laid end to end along the dimension named above; each array names one. Nothing has to cross between parts.
Inputs may be any that keep to these rules, and one draw needn't show every extreme that they name: Every request is cached in its first lengths slots; some request of each group has all 4096 slots filled. `slot_of`: a permutation of the 16 decode slots. `kv`: rows at or beyond a request's length are zero.
All inputs are finite; a program needn't handle non-finite values.
Results may differ from the reference program's by a relative error of at most 0.014.
Values may be sent and summed in bfloat16 or wider, within the bound.
No kernel may reach another device: no remote copies, remote signals or barrier semaphores. Data moves between devices by JAX's collectives and lax.ppermute only.
A program may use at most 128 MiB of HBM per device.

```python
import jax
import jax.numpy as jnp
from jax import lax

H = 128
DL = 512
DK = 576
LMAX = 4096
NEW = 4
R = 16


def shared_ints(key):
    order = jax.random.permutation(jax.random.fold_in(key, 101), R).astype(jnp.int32)
    spans = jax.random.randint(jax.random.fold_in(key, 102), (R,), LMAX // 8, LMAX + 1).astype(jnp.int32)
    chosen = jax.random.randint(jax.random.fold_in(key, 103), (), 0, R)
    spans = jnp.where(jnp.arange(R) == chosen, LMAX, spans).astype(jnp.int32)
    return (order, spans)


def row_normals(key, flat):
    base = jax.random.fold_in(key, 105)
    values = jax.vmap(lambda item: jax.random.normal(jax.random.fold_in(base, item), (DK,), jnp.float32))(flat.reshape(-1))
    return values.reshape(flat.shape + (DK,))


def draw_lengths(key, part):
    order, spans = shared_ints(key)
    return spans


def draw_slot_of(key, part):
    order, spans = shared_ints(key)
    return order


def draw_kv(key, part):
    order, spans = shared_ints(key)
    flat = jnp.arange(R * LMAX, dtype=jnp.int32).reshape(R, LMAX)
    rows = row_normals(key, flat)
    inside = jnp.arange(LMAX)[None, :] < spans[:, None]
    rows = jnp.where(inside[:, :, None], rows, 0.0)
    return rows.astype(jnp.bfloat16)


def draw_query(key, part):
    key_two = jax.random.fold_in(key, 2)
    values = jax.random.normal(key_two, (NEW, R, H, DK), jnp.float32)
    return values.astype(jnp.bfloat16)


def shard_levels(own_key, extent, pieces, least, high):
    def one(dim, parts):
        steps = jax.random.uniform(jax.random.fold_in(jax.random.fold_in(own_key, 6), dim), (parts,), jnp.float32, least / len(pieces), high / len(pieces))
        return jnp.repeat(jnp.exp(steps), extent[dim] // parts).reshape((-1,) + (1,) * (len(extent) - dim - 1))

    level = one(*pieces[0])
    for cut in pieces[1:]:
        level = level * one(*cut)
    return level


def centred(key, dims, width, reach, split=(), kind=jnp.bfloat16):
    entries = jax.random.normal(key, dims, jnp.float32) * width
    if len(split) > 0:
        entries = shard_levels(key, dims, split, -0.22, 0.18) * entries
    return jnp.clip(entries, min=-reach, max=reach).astype(kind)


def setup_inputs(seed: int = 0, part: int = 0) -> dict:
    seeds = jax.random.split(jax.random.key(seed), 6)
    part_splits = jax.random.split(jax.random.fold_in(seeds[5], part), 6)
    return {
        "kv": draw_kv(jax.random.fold_in(jax.random.fold_in(seeds[5], part), 71), part),
        "lengths": draw_lengths(jax.random.fold_in(jax.random.fold_in(seeds[5], part), 71), part),
        "slot_of": draw_slot_of(jax.random.fold_in(jax.random.fold_in(seeds[5], part), 71), part),
        "query": draw_query(jax.random.fold_in(jax.random.fold_in(seeds[5], part), 71), part),
        "new_latent": centred(part_splits[4], (NEW, R, DK), 1.0, 6.0, ((1, 8),)),
    }


score_scale = 192.0 ** -0.5
big_negative = -1e30


def reference(kv, lengths, slot_of, query, new_latent):
    inverse = jnp.zeros((R,), jnp.int32).at[slot_of].set(jnp.arange(R, dtype=jnp.int32))
    owned = jnp.take(kv, inverse, axis=0)
    owned_len = jnp.take(lengths, inverse, axis=0)
    rows = NEW * H
    row_step = jnp.arange(rows, dtype=jnp.int32) // H

    def one_slot(index):
        cache_rows = owned[index]
        fresh = new_latent[:, index]
        queries = query[:, index].reshape(rows, DK)
        valid_one = jnp.arange(LMAX, dtype=jnp.int32)[None, :] < owned_len[index]
        valid_two = jnp.arange(NEW, dtype=jnp.int32)[None, :] <= row_step[:, None]
        cache_scores = jnp.dot(queries, cache_rows.T, preferred_element_type=jnp.float32) * score_scale
        new_scores = jnp.dot(queries, fresh.T, preferred_element_type=jnp.float32) * score_scale
        top = jnp.maximum(jnp.max(jnp.where(valid_one, cache_scores, big_negative), axis=1),
                          jnp.max(jnp.where(valid_two, new_scores, big_negative), axis=1))
        weight_one = jnp.where(valid_one, jnp.exp(cache_scores - top[:, None]), 0.0)
        weight_two = jnp.where(valid_two, jnp.exp(new_scores - top[:, None]), 0.0)
        total = jnp.sum(weight_one, axis=1) + jnp.sum(weight_two, axis=1)
        summed = jnp.dot(weight_one.astype(jnp.bfloat16), cache_rows[:, :DL], preferred_element_type=jnp.float32)
        summed = summed + jnp.dot(weight_two.astype(jnp.bfloat16), fresh[:, :DL], preferred_element_type=jnp.float32)
        return (summed / total[:, None]).astype(jnp.bfloat16).reshape(NEW, H, DL)

    attended = lax.map(one_slot, jnp.arange(R, dtype=jnp.int32))
    return jnp.transpose(attended, (1, 0, 2, 3)), owned
```

```python
import functools

import jax
import jax.numpy as jnp
from jax import lax
from jax.experimental import pallas as pl
from jax.experimental.pallas import tpu as pltpu
from jax.sharding import PartitionSpec as P

DL = 512
CHUNK = 256
LAG = 2
TMAX = 256
UNROLLED = 12
BODY = 4
SLOTS = 160

score_scale = 192.0 ** (-0.5)
big_negative = -1e30

ANY = pl.BlockSpec(memory_space=pl.ANY)
VMEM = pl.BlockSpec(memory_space=pltpu.VMEM)
SMEM = pl.BlockSpec(memory_space=pltpu.SMEM)

SMALL = pltpu.CompilerParams(vmem_limit_bytes=8 * 2**20)

FROM_KV, FROM_PRE, FROM_LINK, FROM_INBOX = 0, 16, 24, 32

SEND, KEEP, LAST, META = 0, 3 * TMAX, 6 * TMAX, 6 * TMAX + 16
N_META = 8
PLAN = META + 2 * N_META + 8


def cdiv(a, b):
    return (a + b - 1) // b


def plan_kernel(zs, where, lengths, slot_of, plan, inbox, busy, load, var):
    me, head = where[0], where[1]
    words = TMAX // 32
    count = 4 * zs
    n_links = 6 * zs
    per_half = 2048 // CHUNK

    def clear(i, _):
        plan[i] = -1
        return 0

    lax.fori_loop(0, PLAN, clear, 0)

    def clear_busy(i, _):
        busy[i] = 0
        return 0

    lax.fori_loop(0, n_links * words, clear_busy, 0)

    def clear_load(i, _):
        load[i] = 0
        return 0

    lax.fori_loop(0, n_links, clear_load, 0)
    var[3] = 0
    var[4] = 0

    def up_link(z, y):
        return z * 2 + y

    def down_link(z, y):
        return 2 * zs + z * 2 + y

    def y_link(z, y):
        return 4 * zs + z * 2 + y

    def place(link, kind, sender, receiver, first_code):
        begin = var[0] + LAG
        word0 = begin >> 5
        free0 = ~busy[link * words + word0] & (jnp.int32(-1) << (begin & 31))

        def full(state):
            return state[1] == 0

        def onward(state):
            word = state[0] + 1
            return word, ~busy[link * words + word]

        word, free = lax.while_loop(full, onward, (word0, free0))
        low = free & -free
        busy[link * words + word] = busy[link * words + word] | low
        time = word * 32 + 31 - lax.clz(low)

        @pl.when(sender == me)
        def _():
            later = jnp.where(time == begin, FROM_LINK + var[1], FROM_INBOX + var[2])
            plan[SEND + time * 3 + kind] = jnp.where(var[0] < 0, first_code, later)

        @pl.when(receiver == me)
        def _():
            plan[KEEP + (time + LAG) * 3 + kind] = var[3]
            var[2] = var[3]
            var[3] = var[3] + 1

        var[0] = time
        var[1] = kind

    def sizes(r):
        n = cdiv(lengths[r], CHUNK)
        return n, cdiv(n, 2)

    def route(r, _):
        src = r // 2
        dst = slot_of[r] // 2
        n, h = sizes(r)
        z0, y0 = src // 2, src % 2
        z1, y1 = dst // 2, dst % 2
        up = z1 > z0
        low, high = jnp.minimum(z0, z1), jnp.maximum(z0, z1)
        offset = jnp.where(up, 0, 2 * zs)

        @pl.when(src != dst)
        def _():
            for part in range(2):
                amount = h // 2 if part == 0 else h - h // 2

                def cost(col):
                    def z_load(z, top):
                        return jnp.maximum(top, load[offset + z * 2 + col])

                    top = lax.fori_loop(low, high, z_load, jnp.int32(0))
                    first = jnp.where(col != y0, load[y_link(z0, y0)], 0)
                    last = jnp.where(col != y1, load[y_link(z1, col)], 0)
                    return jnp.maximum(top, jnp.maximum(first, last))

                straight = cost(y0)
                other = cost(1 - y0)
                take_other = jnp.where(y0 == y1, other + amount < straight, other < straight)
                col = jnp.where((z0 != z1) & take_other, 1 - y0, y0)
                var[8 + 2 * r + part] = col

                def z_add(z, _):
                    load[offset + z * 2 + col] = load[offset + z * 2 + col] + amount
                    return 0

                lax.fori_loop(low, high, z_add, 0)

                @pl.when(col != y0)
                def _():
                    load[y_link(z0, y0)] = load[y_link(z0, y0)] + amount

                @pl.when(col != y1)
                def _():
                    load[y_link(z1, col)] = load[y_link(z1, col)] + amount

        return 0

    lax.fori_loop(0, count, route, 0)

    def stream(r, part, hops):
        src = r // 2
        slot = slot_of[r]
        dst = slot // 2
        n, h = sizes(r)
        z0, y0 = src // 2, src % 2
        z1, y1 = dst // 2, dst % 2
        col = var[8 + 2 * r + part]
        dz = jnp.abs(z1 - z0)
        mine = dz + jnp.where(col != y0, 1, 0) + jnp.where(col != y1, 1, 0)

        @pl.when((src != dst) & (mine == hops))
        def _():
            begin = jnp.where(part == 0, 0, h // 2)
            end = jnp.where(part == 0, h // 2, h)
            item = r % 2

            def chunk(j, _):
                ident = jnp.where(head == 0, j, h + j)
                own = FROM_KV + item * per_half + ident % per_half
                handed = FROM_PRE + item * 4 + ident - jnp.minimum(h, 4)
                code = jnp.where((head == 1) & (ident < per_half), handed, own)
                var[0] = -LAG

                @pl.when(col != y0)
                def _():
                    place(y_link(z0, y0), 2, src, src ^ 1, code)

                def z_hop(k, _):
                    up = z1 > z0
                    z = jnp.where(up, z0 + k, z0 - k)
                    edge = jnp.where(up, z, z - 1)
                    link = jnp.where(up, up_link(edge, col), down_link(edge, col))
                    ahead = jnp.where(up, z + 1, z - 1)
                    place(link, edge % 2, z * 2 + col, ahead * 2 + col, code)
                    return 0

                lax.fori_loop(0, dz, z_hop, 0)

                @pl.when(col != y1)
                def _():
                    place(y_link(z1, col), 2, z1 * 2 + col, dst, code)

                @pl.when(dst == me)
                def _():
                    plan[LAST + (slot % 2) * 8 + j] = var[2]

                var[4] = jnp.maximum(var[4], var[0] + 1)
                return 0

            lax.fori_loop(begin, end, chunk, 0)

    def by_hops(k, _):
        def each(rp, _):
            stream(rp // 2, rp % 2, zs + 1 - k)
            return 0

        lax.fori_loop(0, 2 * count, each, 0)
        return 0

    lax.fori_loop(0, zs + 1, by_hops, 0)

    def slots(r, _):
        @pl.when(slot_of[r] // 2 == me)
        def _():
            at = META + (slot_of[r] % 2) * N_META
            n, h = sizes(r)
            stays = r // 2 == me
            base = jnp.where(head == 0, 0, jnp.where(stays, per_half, h))
            end = jnp.where(
                stays,
                jnp.where(head == 0, jnp.minimum(n, per_half), n),
                jnp.where(head == 0, h, n),
            )
            plan[at] = lengths[r]
            plan[at + 1] = n
            plan[at + 2] = base
            plan[at + 3] = jnp.maximum(end - base, 0)
            plan[at + 4] = jnp.where(stays, r % 2, -1)
            plan[at + 5] = h

        return 0

    lax.fori_loop(0, count, slots, 0)
    plan[META + 2 * N_META] = var[4]


def make_plan(zs, where, lengths, slot_of, width):
    return pl.pallas_call(
        functools.partial(plan_kernel, zs),
        in_specs=[SMEM] * 3,
        out_specs=[SMEM, ANY],
        out_shape=[
            jax.ShapeDtypeStruct((PLAN,), jnp.int32),
            jax.ShapeDtypeStruct((SLOTS, width, CHUNK), jnp.bfloat16),
        ],
        scratch_shapes=[
            pltpu.SMEM((6 * zs * (TMAX // 32),), jnp.int32),
            pltpu.SMEM((6 * zs,), jnp.int32),
            pltpu.SMEM((8 + 8 * zs,), jnp.int32),
        ],
    )(where, lengths, slot_of)


def lanes(index):
    return pl.ds(pl.multiple_of(index * CHUNK, CHUNK), CHUNK)


def hand_kernel(where, lengths, kv, out, sems):
    for start in (True, False):
        for item in range(2):
            n = cdiv(lengths[where[0] * 2 + item], CHUNK)
            first = jnp.minimum(cdiv(n, 2), 4)
            for q in range(4):
                copy = pltpu.make_async_copy(
                    kv.at[item, :, lanes(first + q)],
                    out.at[item, :, pl.ds(q * CHUNK, CHUNK)],
                    sems.at[item * 4 + q],
                )
                if start:
                    copy.start()
                else:
                    copy.wait()


def hand_over(where, lengths, kv):
    return pl.pallas_call(
        hand_kernel,
        in_specs=[SMEM, SMEM, ANY],
        out_specs=VMEM,
        out_shape=pltpu.VMEM((2, kv.shape[1], 4 * CHUNK), kv.dtype),
        scratch_shapes=[pltpu.SemaphoreType.DMA((8,))],
        compiler_params=SMALL,
    )(where, lengths, kv)


def step_kernel(time, plan, kv, pre, *refs):
    arrived, _, sends, inbox, sems = refs[:3], refs[3], refs[4:7], refs[7], refs[8]
    now = time[0]

    def load_from(source, kind):
        return pltpu.make_async_copy(source, sends[kind], sems.at[kind])

    def keep(kind):
        slot = plan[KEEP + now * 3 + kind]
        return slot, pltpu.make_async_copy(
            arrived[kind], inbox.at[jnp.maximum(slot, 0)], sems.at[3 + kind]
        )

    for kind in range(3):
        code = plan[SEND + now * 3 + kind]

        @pl.when((code >= FROM_KV) & (code < FROM_PRE))
        def _():
            load_from(kv.at[code >> 3, :, lanes(code & 7)], kind).start()

        @pl.when((code >= FROM_PRE) & (code < FROM_LINK))
        def _():
            load_from(pre.at[(code - FROM_PRE) >> 2, :, lanes(code & 3)], kind).start()

        for other in range(3):

            @pl.when(code == FROM_LINK + other)
            def _():
                load_from(arrived[other], kind).start()

        @pl.when(code >= FROM_INBOX)
        def _():
            load_from(inbox.at[code - FROM_INBOX], kind).start()

    for kind in range(3):
        slot, copy = keep(kind)

        @pl.when(slot >= 0)
        def _():
            copy.start()

    for kind in range(3):

        @pl.when(plan[SEND + now * 3 + kind] >= 0)
        def _():
            load_from(arrived[kind], kind).wait()

        slot, copy = keep(kind)

        @pl.when(slot >= 0)
        def _():
            copy.wait()


def in_vmem(arrays):
    return [pltpu.with_memory_space_constraint(a, pltpu.VMEM) for a in arrays]


def one_step(time, plan, kv, pre, arrived, inbox):
    piece = pltpu.VMEM(inbox.shape[1:], inbox.dtype)
    *sends, inbox = pl.pallas_call(
        step_kernel,
        in_specs=[SMEM, SMEM, ANY, ANY] + [VMEM] * 3 + [ANY],
        out_specs=[VMEM] * 3 + [ANY],
        out_shape=[piece] * 3 + [jax.ShapeDtypeStruct(inbox.shape, inbox.dtype)],
        input_output_aliases={7: 3},
        scratch_shapes=[pltpu.SemaphoreType.DMA((6,))],
        compiler_params=SMALL,
        cost_estimate=pl.CostEstimate(
            flops=0, bytes_accessed=12 * inbox.shape[1] * CHUNK, transcendentals=0
        ),
    )(time, plan, kv, pre, *in_vmem(arrived), inbox)
    return sends, inbox


def finish_kernel(time, plan, *refs):
    arrived, _, inbox, post, sems = refs[:6], refs[6], refs[7], refs[8], refs[9]
    now = time[0]

    for start in (True, False):
        for late in range(LAG):
            for kind in range(3):
                slot = plan[KEEP + (now + late) * 3 + kind]
                copy = pltpu.make_async_copy(
                    arrived[3 * late + kind],
                    inbox.at[jnp.maximum(slot, 0)],
                    sems.at[3 * late + kind],
                )

                @pl.when(slot >= 0)
                def _():
                    if start:
                        copy.start()
                    else:
                        copy.wait()

    per_half = 2048 // CHUNK
    for start in (True, False):
        for item in range(2):
            at = META + item * N_META
            n, base, stays = plan[at + 1], plan[at + 2], plan[at + 4]
            for q in range(4):
                slot = plan[LAST + item * 8 + q]
                copy = pltpu.make_async_copy(
                    inbox.at[jnp.maximum(slot, 0)],
                    post.at[item, :, pl.ds(q * CHUNK, CHUNK)],
                    sems.at[6 + item * 4 + q],
                )

                @pl.when((stays < 0) & (base > 0) & (base + q < jnp.minimum(n, per_half)))
                def _():
                    if start:
                        copy.start()
                    else:
                        copy.wait()


def finish(time, plan, arrived, inbox):
    return pl.pallas_call(
        finish_kernel,
        in_specs=[SMEM, SMEM] + [VMEM] * 6 + [ANY],
        out_specs=[ANY, VMEM],
        out_shape=[
            jax.ShapeDtypeStruct(inbox.shape, inbox.dtype),
            pltpu.VMEM((2, inbox.shape[1], 4 * CHUNK), inbox.dtype),
        ],
        input_output_aliases={8: 0},
        scratch_shapes=[pltpu.SemaphoreType.DMA((14,))],
        compiler_params=SMALL,
    )(time, plan, *in_vmem(arrived), inbox)


def nt_dot(a, b):
    return lax.dot_general(a, b, (((1,), (1,)), ((), ())), preferred_element_type=jnp.float32)


def attend_kernel(
    where, plan, query, query_other, fresh, kv, inbox,
    own_sum, other_sum, stats, cache,
    keys, scores, queries, total, zeros, sems_in, sems_out,
):
    head = where[1]
    per_half = 2048 // CHUNK
    steps, _, heads, _ = query.shape
    own_rows = steps * heads
    rows = 2 * own_rows
    zeros[...] = jnp.zeros_like(zeros)

    def numbers(item):
        at = META + item * N_META
        return [plan[at + k] for k in range(6)]

    def fetch(item, j, start):
        length, n, base, held, stays, h = numbers(item)
        slot = plan[LAST + item * 8 + j]
        place = keys.at[item, :, pl.ds(j * CHUNK, CHUNK)]
        sem = sems_in.at[item * 8 + j]

        @pl.when(stays >= 0)
        def _():
            copy = pltpu.make_async_copy(
                kv.at[jnp.maximum(stays, 0), :, pl.ds(j * CHUNK, CHUNK)], place, sem
            )
            copy.start() if start else copy.wait()

        @pl.when((stays < 0) & (j < held))
        def _():
            copy = pltpu.make_async_copy(inbox.at[jnp.maximum(slot, 0)], place, sem)
            copy.start() if start else copy.wait()

    def store(item, c, start):
        length, n, base, held, stays, h = numbers(item)
        ident = head * per_half + c
        j = ident - base
        place = cache.at[item, :, pl.ds(c * CHUNK, CHUNK)]
        sem = sems_out.at[item * 8 + c]

        @pl.when((j >= 0) & (j < held))
        def _():
            copy = pltpu.make_async_copy(keys.at[item, :, lanes(jnp.maximum(j, 0))], place, sem)
            copy.start() if start else copy.wait()

        @pl.when(ident >= n)
        def _():
            copy = pltpu.make_async_copy(zeros, place, sem)
            copy.start() if start else copy.wait()

    for item in range(2):
        for j in range(per_half):
            fetch(item, j, True)

    for item in range(2):
        length, n, base, held, stays, h = numbers(item)
        for step in range(steps):
            queries[pl.ds(step * heads, heads), :] = query[step, item]
            queries[pl.ds(own_rows + step * heads, heads), :] = query_other[step, item]
        new = fresh[item]
        step_of = lax.broadcasted_iota(jnp.int32, (own_rows, new.shape[0]), 0) // heads
        position = lax.broadcasted_iota(jnp.int32, (own_rows, new.shape[0]), 1)
        valid_new = position <= step_of
        new_scores = nt_dot(queries[pl.ds(0, own_rows), :], new) * score_scale
        new_scores = jnp.where(valid_new, new_scores, big_negative)
        top = jnp.concatenate(
            [
                jnp.max(new_scores, axis=1, keepdims=True),
                jnp.full((rows - own_rows, 1), big_negative, jnp.float32),
            ],
            axis=0,
        )
        for j in range(per_half):
            fetch(item, j, False)
        for c in range(per_half):
            store(item, c, True)

        left = length - base * CHUNK

        def score(j, top):
            part = jnp.dot(
                queries[...], keys[item, :, lanes(j)], preferred_element_type=jnp.float32
            )
            where_ = j * CHUNK + lax.broadcasted_iota(jnp.int32, (rows, CHUNK), 1)
            part = jnp.where(where_ < left, part * score_scale, big_negative)
            scores[:, lanes(j)] = part
            return jnp.maximum(top, jnp.max(part, axis=1, keepdims=True))

        top = lax.fori_loop(0, held, score, top)
        own_top = top[:own_rows]
        new_weight = jnp.where(valid_new, jnp.exp(new_scores - own_top), 0.0)
        total[pl.ds(0, own_rows), :] = jnp.dot(
            new_weight.astype(jnp.bfloat16), new[:, :DL], preferred_element_type=jnp.float32
        )
        total[pl.ds(own_rows, rows - own_rows), :] = jnp.zeros(
            (rows - own_rows, DL), jnp.float32
        )
        weight_sum = jnp.concatenate(
            [
                jnp.sum(new_weight, axis=1, keepdims=True),
                jnp.zeros((rows - own_rows, 1), jnp.float32),
            ],
            axis=0,
        )

        def attend(j, weight_sum):
            where_ = j * CHUNK + lax.broadcasted_iota(jnp.int32, (rows, CHUNK), 1)
            weight = jnp.where(where_ < left, jnp.exp(scores[:, lanes(j)] - top), 0.0)
            total[...] += nt_dot(weight.astype(jnp.bfloat16), keys[item, pl.ds(0, DL), lanes(j)])
            return weight_sum + jnp.sum(weight, axis=1, keepdims=True)

        weight_sum = lax.fori_loop(0, held, attend, weight_sum)
        own_sum[item] = total[pl.ds(0, own_rows), :]
        other_sum[item] = total[pl.ds(own_rows, rows - own_rows), :].astype(jnp.bfloat16)
        lane = lax.broadcasted_iota(jnp.int32, (rows, 128), 1)
        stats[item] = jnp.where(lane == 0, top, weight_sum)

    for item in range(2):
        for c in range(per_half):
            store(item, c, False)


def attend(where, plan, query, query_other, fresh, kv, inbox):
    steps, items, heads, width = query.shape
    own = steps * heads
    return pl.pallas_call(
        attend_kernel,
        in_specs=[SMEM, SMEM, VMEM, VMEM, VMEM, ANY, ANY],
        out_specs=[VMEM, VMEM, VMEM, ANY],
        out_shape=[
            jax.ShapeDtypeStruct((items, own, DL), jnp.float32),
            jax.ShapeDtypeStruct((items, own, DL), jnp.bfloat16),
            jax.ShapeDtypeStruct((items, 2 * own, 128), jnp.float32),
            jax.ShapeDtypeStruct(kv.shape, kv.dtype),
        ],
        scratch_shapes=[
            pltpu.VMEM(kv.shape, kv.dtype),
            pltpu.VMEM((2 * own, kv.shape[2]), jnp.float32),
            pltpu.VMEM((2 * own, width), kv.dtype),
            pltpu.VMEM((2 * own, DL), jnp.float32),
            pltpu.VMEM((width, CHUNK), kv.dtype),
            pltpu.SemaphoreType.DMA((16,)),
            pltpu.SemaphoreType.DMA((16,)),
        ],
        compiler_params=pltpu.CompilerParams(vmem_limit_bytes=48 * 2**20),
    )(where, plan, query, query_other, fresh, kv, inbox)


def return_kernel(where, plan, post, _, cache, sems):
    per_half = 2048 // CHUNK
    for start in (True, False):
        for item in range(2):
            at = META + item * N_META
            n, stays, h = plan[at + 1], plan[at + 4], plan[at + 5]
            for q in range(4):

                @pl.when((where[1] == 0) & (stays < 0) & (h + q < jnp.minimum(n, per_half)))
                def _():
                    copy = pltpu.make_async_copy(
                        post.at[item, :, pl.ds(q * CHUNK, CHUNK)],
                        cache.at[item, :, lanes(jnp.minimum(h + q, per_half - 1))],
                        sems.at[item * 4 + q],
                    )
                    copy.start() if start else copy.wait()


def return_rows(where, plan, post, cache):
    return pl.pallas_call(
        return_kernel,
        in_specs=[SMEM, SMEM, ANY, ANY],
        out_specs=ANY,
        out_shape=jax.ShapeDtypeStruct(cache.shape, cache.dtype),
        input_output_aliases={3: 0},
        scratch_shapes=[pltpu.SemaphoreType.DMA((8,))],
    )(where, plan, post, cache)


def merge_kernel(own_sum, stats, other_sum, other_stats, out):
    items, own, _ = own_sum.shape
    steps, _, heads, _ = out.shape
    for item in range(items):
        one = stats[item, pl.ds(0, own), :]
        two = other_stats[item]
        top = jnp.maximum(one[:, :1], two[:, :1])
        scale_one = jnp.exp(one[:, :1] - top)
        scale_two = jnp.exp(two[:, :1] - top)
        total = one[:, 1:2] * scale_one + two[:, 1:2] * scale_two
        summed = own_sum[item] * scale_one + other_sum[item].astype(jnp.float32) * scale_two
        result = (summed / total).astype(out.dtype)
        for step in range(steps):
            out[step, item] = result[step * heads : (step + 1) * heads]


def merge(own_sum, stats, other_sum, other_stats, steps, heads):
    return pl.pallas_call(
        merge_kernel,
        in_specs=[VMEM] * 4,
        out_specs=VMEM,
        out_shape=jax.ShapeDtypeStruct((steps, own_sum.shape[0], heads, DL), jnp.bfloat16),
    )(own_sum, stats, other_sum, other_stats)


def exchanges(zs):
    even, odd, across = [], [], []
    for z in range(zs):
        for y in range(2):
            across.append((z * 2 + y, z * 2 + 1 - y))
            if z + 1 < zs:
                pairs = even if z % 2 == 0 else odd
                pairs.append((z * 2 + y, z * 2 + 2 + y))
                pairs.append((z * 2 + 2 + y, z * 2 + y))
    return even, odd, across


def routed(zs, kv, lengths, slot_of, query, new_latent):
    kinds = exchanges(zs)
    steps, items, heads, width = query.shape
    where = jnp.stack([lax.axis_index("seq"), lax.axis_index("head")]).astype(jnp.int32)
    kv = jnp.swapaxes(kv, 1, 2)
    swap = [(0, 1), (1, 0)]
    pre = lax.ppermute(hand_over(where, lengths, kv), "head", [(0, 1)])
    query_other = lax.ppermute(query, "head", swap)
    fresh = jnp.pad(jnp.swapaxes(new_latent, 0, 1), ((0, 0), (0, 128 - steps), (0, 0)))
    plan, inbox = make_plan(zs, where, lengths, slot_of, width)
    last_step = plan[META + 2 * N_META]

    def step(time, arrived, inbox):
        sends, inbox = one_step(jnp.full((1,), time, jnp.int32), plan, kv, pre, arrived, inbox)
        return [lax.ppermute(s, "seq", k) for s, k in zip(sends, kinds)], inbox

    def run(begin, count, arrived, inbox):
        for k in range(count):
            new, inbox = step(begin + k, arrived[0], inbox)
            arrived = [arrived[1], new]
        return arrived, inbox

    nothing = [jnp.zeros((width, CHUNK), kv.dtype)] * 3
    arrived, inbox = run(0, UNROLLED, [nothing, nothing], inbox)

    def more(state):
        return state[0] < last_step

    def body(state):
        time, arrived, inbox = state
        arrived, inbox = run(time, BODY, arrived, inbox)
        return time + BODY, arrived, inbox

    time, arrived, inbox = lax.while_loop(more, body, (jnp.int32(UNROLLED), arrived, inbox))
    inbox, post = finish(time[None], plan, arrived[0] + arrived[1], inbox)
    post = lax.ppermute(post, "head", [(1, 0)])
    own_sum, other_sum, stats, cache = attend(
        where, plan, query, query_other, fresh, kv, inbox
    )
    other_sum = lax.ppermute(other_sum, "head", swap)
    other_stats = lax.ppermute(stats[:, steps * heads :], "head", swap)
    cache = return_rows(where, plan, post, cache)
    attended = merge(own_sum, stats, other_sum, other_stats, steps, heads)
    return attended, jnp.swapaxes(cache, 1, 2)


def merged_2(shard, axis, combine):
    everything = jax.tree.map(
        lambda part, kind: lax.all_gather(part.astype(kind), axis),
        shard,
        (jnp.bfloat16, jnp.bfloat16, jnp.bfloat16),
    )

    def take(k):
        return jax.tree.map(lambda part, own: part[k].astype(own.dtype), everything, shard)

    return lax.fori_loop(
        1, lax.axis_size(axis), lambda k, so_far: combine(so_far, take(k)), take(0)
    )


def join_partials(first, second):
    top = jnp.maximum(first[0], second[0])
    scale_one = jnp.exp(first[0] - top)
    scale_two = jnp.exp(second[0] - top)
    total = first[1] * scale_one + second[1] * scale_two
    summed = first[2] * scale_one[..., None] + second[2] * scale_two[..., None]
    return (top, total, summed)


def balanced(kv, lengths, slot_of, query, new_latent):
    req = kv.shape[0]
    half = kv.shape[1]
    count = lengths.shape[0]
    steps_new = query.shape[0]
    heads_here = query.shape[2]
    pieces = lax.all_to_all(kv, "seq", split_axis=1, concat_axis=0, tiled=True)
    inverse = jnp.zeros((count,), jnp.int32).at[slot_of].set(jnp.arange(count, dtype=jnp.int32))
    ordered = jnp.take(pieces, inverse, axis=0)
    cache = lax.all_to_all(ordered, "seq", split_axis=0, concat_axis=1, tiled=True)
    my_lens = lax.dynamic_slice_in_dim(
        jnp.take(lengths, inverse, axis=0), lax.axis_index("seq") * req, req
    )
    head_pos = lax.axis_index("head")
    rows = steps_new * heads_here
    row_step = jnp.arange(rows, dtype=jnp.int32) // heads_here
    valid_two = jnp.arange(steps_new, dtype=jnp.int32)[None, :] <= row_step[:, None]
    results = []
    every_query = lax.all_gather(query, "head", axis=2, tiled=True)
    heads_all = every_query.shape[2]
    rows_all = steps_new * heads_all
    positions = head_pos * half + jnp.arange(half, dtype=jnp.int32)
    tops = []
    totals = []
    sums = []
    for item in range(req):
        queries = every_query[:, item].reshape(rows_all, every_query.shape[3])
        valid_one = positions[None, :] < my_lens[item]
        cache_scores = (
            jnp.einsum("nd,td->nt", queries, cache[item], preferred_element_type=jnp.float32)
            * score_scale
        )
        top = jnp.max(jnp.where(valid_one, cache_scores, big_negative), axis=1)
        weight_one = jnp.where(valid_one, jnp.exp(cache_scores - top[:, None]), 0.0)
        tops.append(top)
        totals.append(jnp.sum(weight_one, axis=1))
        sums.append(
            jnp.dot(
                weight_one.astype(jnp.bfloat16),
                cache[item][:, :DL],
                preferred_element_type=jnp.float32,
            )
        )
    merged = merged_2((jnp.stack(tops), jnp.stack(totals), jnp.stack(sums)), "head", join_partials)
    start = head_pos * heads_here
    own_top = lax.dynamic_slice_in_dim(
        merged[0].reshape(req, steps_new, heads_all), start, heads_here, 2
    ).reshape(req, rows)
    own_total = lax.dynamic_slice_in_dim(
        merged[1].reshape(req, steps_new, heads_all), start, heads_here, 2
    ).reshape(req, rows)
    own_sum = lax.dynamic_slice_in_dim(
        merged[2].reshape(req, steps_new, heads_all, DL), start, heads_here, 2
    ).reshape(req, rows, DL)
    for item in range(req):
        queries = query[:, item].reshape(rows, query.shape[3])
        fresh = new_latent[:, item]
        new_scores = (
            jnp.einsum("nd,td->nt", queries, fresh, preferred_element_type=jnp.float32)
            * score_scale
        )
        top = jnp.maximum(
            own_top[item], jnp.max(jnp.where(valid_two, new_scores, big_negative), axis=1)
        )
        rescale = jnp.exp(own_top[item] - top)
        weight_two = jnp.where(valid_two, jnp.exp(new_scores - top[:, None]), 0.0)
        total = own_total[item] * rescale + jnp.sum(weight_two, axis=1)
        summed = own_sum[item] * rescale[:, None]
        summed = summed + jnp.dot(
            weight_two.astype(jnp.bfloat16), fresh[:, :DL], preferred_element_type=jnp.float32
        )
        results.append(
            (summed / total[:, None]).astype(jnp.bfloat16).reshape(steps_new, heads_here, DL)
        )
    return (jnp.stack(results, axis=1), cache)


def solution(mesh):
    local = functools.partial(routed, 4) if mesh.shape["seq"] == 8 else balanced
    return jax.shard_map(
        local,
        mesh=mesh,
        in_specs=(
            P(("groups", "seq"), "head", None),
            P("groups"),
            P("groups"),
            P(None, ("groups", "seq"), "head", None),
            P(None, ("groups", "seq"), None),
        ),
        out_specs=(P(None, ("groups", "seq"), "head", None), P(("groups", "seq"), "head", None)),
        check_vma=False,
    )
```

```python
import functools

import jax
import jax.numpy as jnp
from jax import lax
from jax.experimental import pallas as pl
from jax.experimental.pallas import tpu as pltpu
from jax.sharding import PartitionSpec as P

DL = 512
CHUNK_BITS = 8
CHUNK = 1 << CHUNK_BITS
LAG = 2
TMAX = 256
UNROLLED = 12
BODY = 4
SLOTS = 160

score_scale = 192.0 ** (-0.5)
big_negative = -1e30

ANY = pl.BlockSpec(memory_space=pl.ANY)
VMEM = pl.BlockSpec(memory_space=pltpu.VMEM)
SMEM = pl.BlockSpec(memory_space=pltpu.SMEM)

SMALL = pltpu.CompilerParams(vmem_limit_bytes=8 * 2**20)

FROM_KV, FROM_PRE, FROM_LINK, FROM_INBOX, NOTHING = 0, 16, 24, 32, 255

SEND, KEEP, LAST, META = 0, TMAX, 2 * TMAX, 2 * TMAX + 16
N_META = 8
PLAN = META + 2 * N_META + 8


def cdiv(a, b):
    return (a + b - 1) // b


def plan_kernel(zs, where, lengths, slot_of, plan, inbox, busy, load, bucket, var):
    me, head = where[0], where[1]
    words = TMAX // 32
    count = 4 * zs
    per_half = 2048 // CHUNK
    streams = 2 * count

    def fill(ref, begin, size, value):
        wide = 16
        assert size % wide == 0

        def some(i, _):
            for k in range(wide):
                ref[begin + i * wide + k] = value
            return 0

        lax.fori_loop(0, size // wide, some, 0)

    fill(plan, 0, 2 * TMAX, jnp.int32(-1))
    fill(busy, 0, 6 * zs * words, jnp.int32(0))
    for i in range(6 * zs):
        load[i] = 0
    for i in range(zs + 2):
        var[i] = 0
    var[zs + 2] = 0
    var[zs + 3] = 0

    def y_link(z, y):
        return 4 * zs + z * 2 + y

    def sizes(r):
        n = (lengths[r] + CHUNK - 1) >> CHUNK_BITS
        return n, (n + 1) >> 1

    def route(r, _):
        src = r >> 1
        dst = slot_of[r] >> 1
        n, h = sizes(r)
        z0, y0 = src >> 1, src & 1
        z1, y1 = dst >> 1, dst & 1
        low, high = jnp.minimum(z0, z1), jnp.maximum(z0, z1)
        offset = jnp.where(z1 > z0, 0, 2 * zs)
        inside = [(low <= z) & (z < high) for z in range(zs - 1)]
        turn = jnp.where(y0 == y1, 0, 1)
        for part in range(2):
            amount = jnp.where(src == dst, 0, h >> 1 if part == 0 else h - (h >> 1))

            def cost(col):
                top = jnp.int32(0)
                for z in range(zs - 1):
                    top = jnp.maximum(top, jnp.where(inside[z], load[offset + z * 2 + col], 0))
                return top

            straight = jnp.maximum(cost(y0), jnp.where(turn == 1, load[y_link(z1, y0)], 0))
            other = jnp.maximum(cost(1 - y0), load[y_link(z0, y0)])
            other = jnp.where(
                turn == 1, other, jnp.maximum(other, load[y_link(z1, 1 - y0)]) + amount
            )
            col = jnp.where((z0 != z1) & (other < straight), 1 - y0, y0)
            for z in range(zs - 1):
                at = offset + z * 2 + col
                load[at] = load[at] + jnp.where(inside[z], amount, 0)
            first = jnp.where(col != y0, 1, 0)
            last = jnp.where(col != y1, 1, 0)
            at = y_link(z0, y0)
            load[at] = load[at] + first * amount
            at = y_link(z1, col)
            load[at] = load[at] + last * amount
            hops = jnp.where(amount == 0, 0, high - low + first + last)
            filled = var[hops]
            bucket[hops * streams + filled] = r * 4 + part * 2 + col
            var[hops] = filled + 1
        return 0

    lax.fori_loop(0, count, route, 0)

    def stream(hops, index):
        packed = bucket[hops * streams + index]
        r, part, col = packed >> 2, (packed >> 1) & 1, packed & 1
        src = r >> 1
        slot = slot_of[r]
        dst = slot >> 1
        n, h = sizes(r)
        half = h >> 1
        begin = jnp.where(part == 0, 0, half)
        amount = jnp.where(part == 0, half, h - half)
        item = r & 1
        z0, y0 = src >> 1, src & 1
        z1 = dst >> 1
        up = jnp.where(z1 > z0, 1, 0)
        sign = 2 * up - 1
        first = jnp.where(col != y0, 1, 0)
        dz = jnp.abs(z1 - z0)

        def hop(i, state):
            times, kind_before, slot_before = state[:4], state[4], state[5]
            is_first = i < first
            is_last = i >= first + dz
            z = z0 + sign * (i - first)
            edge = z + up - 1
            is_y = is_first | is_last
            z_turn = jnp.where(is_first, z0, z1)
            y_from = jnp.where(is_first, y0, col)
            link = jnp.where(
                is_y, y_link(z_turn, y_from), jnp.where(up == 1, 0, 2 * zs) + edge * 2 + col
            )
            kind = jnp.where(is_y, 2, edge & 1)
            sender = jnp.where(is_y, z_turn, z) * 2 + y_from
            sender = jnp.where(is_y, sender, z * 2 + col)
            receiver = jnp.where(is_y, z_turn * 2 + 1 - y_from, (z + sign) * 2 + col)
            row = link * words
            new_times = []
            for j in range(4):
                start = times[j] + LAG
                word0 = start >> 5
                free0 = ~busy[row + word0] & (jnp.int32(-1) << (start & 31))

                def onward(state):
                    word = state[0] + 1
                    return word, ~busy[row + word]

                word, free = lax.while_loop(lambda s: s[1] == 0, onward, (word0, free0))
                low = jnp.where(j < amount, free & -free, 0)
                busy[row + word] = busy[row + word] | low
                new_times.append(word * 32 + 31 - lax.clz(free & -free))
            slot_now = var[zs + 2]

            @pl.when((sender == me) | (receiver == me))
            def _():
                shift = kind * 8
                for j in range(4):
                    ident = begin + j + jnp.where(head == 0, 0, h)
                    own = FROM_KV + item * per_half + (ident & (per_half - 1))
                    handed = FROM_PRE + item * 4 + ident - jnp.minimum(h, 4)
                    code = jnp.where((head == 1) & (ident < per_half), handed, own)
                    passed = jnp.where(
                        new_times[j] == times[j] + LAG,
                        FROM_LINK + kind_before,
                        FROM_INBOX + slot_before + j,
                    )
                    code = jnp.where(i == 0, code, passed)
                    here = (sender == me) & (j < amount)
                    at = SEND + new_times[j]
                    plan[at] = plan[at] ^ jnp.where(here, (code ^ 255) << shift, 0)
                    here = (receiver == me) & (j < amount)
                    at = KEEP + new_times[j] + LAG
                    plan[at] = plan[at] ^ jnp.where(here, ((slot_now + j) ^ 255) << shift, 0)
                var[zs + 2] = slot_now + jnp.where(receiver == me, amount, 0)

            return (*new_times, kind, slot_now)

        early = jnp.int32(-LAG)
        state = lax.fori_loop(0, hops, hop, (early, early, early, early, jnp.int32(0), jnp.int32(0)))
        end = jnp.maximum(jnp.maximum(state[0], state[1]), jnp.maximum(state[2], state[3]))
        for j in range(4):
            end = jnp.where(j == amount - 1, state[j], end)
        var[zs + 3] = jnp.maximum(var[zs + 3], end + 1)

        @pl.when(dst == me)
        def _():
            for j in range(4):
                plan[LAST + (slot & 1) * 8 + part * 4 + j] = state[5] + j

    def by_hops(k, _):
        hops = zs + 1 - k

        def each(index, _):
            stream(hops, index)
            return 0

        lax.fori_loop(0, var[hops], each, 0)
        return 0

    lax.fori_loop(0, zs + 1, by_hops, 0)

    def slots(r, _):
        @pl.when(slot_of[r] >> 1 == me)
        def _():
            at = META + (slot_of[r] & 1) * N_META
            n, h = sizes(r)
            stays = r >> 1 == me
            base = jnp.where(head == 0, 0, jnp.where(stays, per_half, h))
            end = jnp.where(
                stays,
                jnp.where(head == 0, jnp.minimum(n, per_half), n),
                jnp.where(head == 0, h, n),
            )
            plan[at] = lengths[r]
            plan[at + 1] = n
            plan[at + 2] = base
            plan[at + 3] = jnp.maximum(end - base, 0)
            plan[at + 4] = jnp.where(stays, r & 1, -1)
            plan[at + 5] = h

        return 0

    lax.fori_loop(0, count, slots, 0)
    plan[META + 2 * N_META] = var[zs + 3]


def make_plan(zs, where, lengths, slot_of, width):
    return pl.pallas_call(
        functools.partial(plan_kernel, zs),
        in_specs=[SMEM] * 3,
        out_specs=[SMEM, ANY],
        out_shape=[
            jax.ShapeDtypeStruct((PLAN,), jnp.int32),
            jax.ShapeDtypeStruct((SLOTS, width, CHUNK), jnp.bfloat16),
        ],
        scratch_shapes=[
            pltpu.SMEM((6 * zs * (TMAX // 32),), jnp.int32),
            pltpu.SMEM((6 * zs,), jnp.int32),
            pltpu.SMEM(((zs + 2) * 8 * zs,), jnp.int32),
            pltpu.SMEM((zs + 4,), jnp.int32),
        ],
    )(where, lengths, slot_of)


def lanes(index):
    return pl.ds(pl.multiple_of(index * CHUNK, CHUNK), CHUNK)


def hand_kernel(where, lengths, kv, out, sems):
    for start in (True, False):
        for item in range(2):
            n = cdiv(lengths[where[0] * 2 + item], CHUNK)
            first = jnp.minimum(cdiv(n, 2), 4)
            for q in range(4):
                copy = pltpu.make_async_copy(
                    kv.at[item, :, lanes(first + q)],
                    out.at[item, :, pl.ds(q * CHUNK, CHUNK)],
                    sems.at[item * 4 + q],
                )
                if start:
                    copy.start()
                else:
                    copy.wait()


def hand_over(where, lengths, kv):
    return pl.pallas_call(
        hand_kernel,
        in_specs=[SMEM, SMEM, ANY],
        out_specs=VMEM,
        out_shape=pltpu.VMEM((2, kv.shape[1], 4 * CHUNK), kv.dtype),
        scratch_shapes=[pltpu.SemaphoreType.DMA((8,))],
        compiler_params=SMALL,
    )(where, lengths, kv)


def step_kernel(time, plan, kv, pre, *refs):
    arrived, _, sends, inbox, sems = refs[:3], refs[3], refs[4:7], refs[7], refs[8]
    to_send, to_keep = plan[SEND + time[0]], plan[KEEP + time[0]]
    codes = [(to_send >> (8 * kind)) & 255 for kind in range(3)]
    slots = [(to_keep >> (8 * kind)) & 255 for kind in range(3)]

    def load_from(source, kind):
        return pltpu.make_async_copy(source, sends[kind], sems.at[kind])

    def keep(kind):
        return pltpu.make_async_copy(
            arrived[kind], inbox.at[jnp.minimum(slots[kind], SLOTS - 1)], sems.at[3 + kind]
        )

    for kind in range(3):
        code = codes[kind]

        @pl.when(code < FROM_PRE)
        def _():
            load_from(kv.at[code >> 3, :, lanes(code & 7)], kind).start()

        @pl.when((code >= FROM_PRE) & (code < FROM_LINK))
        def _():
            load_from(pre.at[(code - FROM_PRE) >> 2, :, lanes(code & 3)], kind).start()

        for other in range(3):

            @pl.when(code == FROM_LINK + other)
            def _():
                load_from(arrived[other], kind).start()

        @pl.when((code >= FROM_INBOX) & (code < NOTHING))
        def _():
            load_from(inbox.at[code - FROM_INBOX], kind).start()

        @pl.when(slots[kind] < NOTHING)
        def _():
            keep(kind).start()

    for kind in range(3):

        @pl.when(codes[kind] < NOTHING)
        def _():
            load_from(arrived[kind], kind).wait()

        @pl.when(slots[kind] < NOTHING)
        def _():
            keep(kind).wait()


def in_vmem(arrays):
    return [pltpu.with_memory_space_constraint(a, pltpu.VMEM) for a in arrays]


def one_step(time, plan, kv, pre, arrived, inbox):
    piece = pltpu.VMEM(inbox.shape[1:], inbox.dtype)
    *sends, inbox = pl.pallas_call(
        step_kernel,
        in_specs=[SMEM, SMEM, ANY, ANY] + [VMEM] * 3 + [ANY],
        out_specs=[VMEM] * 3 + [ANY],
        out_shape=[piece] * 3 + [jax.ShapeDtypeStruct(inbox.shape, inbox.dtype)],
        input_output_aliases={7: 3},
        scratch_shapes=[pltpu.SemaphoreType.DMA((6,))],
        compiler_params=SMALL,
        cost_estimate=pl.CostEstimate(
            flops=0, bytes_accessed=12 * inbox.shape[1] * CHUNK, transcendentals=0
        ),
    )(time, plan, kv, pre, *in_vmem(arrived), inbox)
    return sends, inbox


def slot_of_chunk(plan, item, j, h, stays):
    half = h >> 1
    at = jnp.where(j < half, j, jnp.minimum(4 + j - half, 7))
    return jnp.where((stays < 0) & (j < h), plan[LAST + item * 8 + at], 0)


def finish_kernel(time, plan, *refs):
    arrived, _, inbox, post, sems = refs[:6], refs[6], refs[7], refs[8], refs[9]
    now = time[0]

    for start in (True, False):
        for late in range(LAG):
            for kind in range(3):
                slot = (plan[KEEP + now + late] >> (8 * kind)) & 255
                copy = pltpu.make_async_copy(
                    arrived[3 * late + kind],
                    inbox.at[jnp.minimum(slot, SLOTS - 1)],
                    sems.at[3 * late + kind],
                )

                @pl.when(slot < NOTHING)
                def _():
                    if start:
                        copy.start()
                    else:
                        copy.wait()

    per_half = 2048 // CHUNK
    for start in (True, False):
        for item in range(2):
            at = META + item * N_META
            n, base, stays, h = plan[at + 1], plan[at + 2], plan[at + 4], plan[at + 5]
            for q in range(4):
                copy = pltpu.make_async_copy(
                    inbox.at[slot_of_chunk(plan, item, q, h, stays)],
                    post.at[item, :, pl.ds(q * CHUNK, CHUNK)],
                    sems.at[6 + item * 4 + q],
                )

                @pl.when((stays < 0) & (base > 0) & (base + q < jnp.minimum(n, per_half)))
                def _():
                    if start:
                        copy.start()
                    else:
                        copy.wait()


def finish(time, plan, arrived, inbox):
    return pl.pallas_call(
        finish_kernel,
        in_specs=[SMEM, SMEM] + [VMEM] * 6 + [ANY],
        out_specs=[ANY, VMEM],
        out_shape=[
            jax.ShapeDtypeStruct(inbox.shape, inbox.dtype),
            pltpu.VMEM((2, inbox.shape[1], 4 * CHUNK), inbox.dtype),
        ],
        input_output_aliases={8: 0},
        scratch_shapes=[pltpu.SemaphoreType.DMA((14,))],
        compiler_params=SMALL,
    )(time, plan, *in_vmem(arrived), inbox)


def nt_dot(a, b):
    return lax.dot_general(a, b, (((1,), (1,)), ((), ())), preferred_element_type=jnp.float32)


def attend_kernel(
    where, plan, query, query_other, fresh, kv, inbox,
    own_sum, other_sum, stats, cache,
    keys, scores, queries, total, zeros, sems_in, sems_out,
):
    head = where[1]
    per_half = 2048 // CHUNK
    steps, _, heads, _ = query.shape
    own_rows = steps * heads
    rows = 2 * own_rows
    zeros[...] = jnp.zeros_like(zeros)

    def numbers(item):
        at = META + item * N_META
        return [plan[at + k] for k in range(6)]

    def fetch(item, j, start):
        length, n, base, held, stays, h = numbers(item)
        place = keys.at[item, :, pl.ds(j * CHUNK, CHUNK)]
        sem = sems_in.at[item * 8 + j]

        @pl.when(stays >= 0)
        def _():
            copy = pltpu.make_async_copy(
                kv.at[jnp.maximum(stays, 0), :, pl.ds(j * CHUNK, CHUNK)], place, sem
            )
            copy.start() if start else copy.wait()

        @pl.when((stays < 0) & (j < held))
        def _():
            slot = slot_of_chunk(plan, item, j, h, stays)
            copy = pltpu.make_async_copy(inbox.at[slot], place, sem)
            copy.start() if start else copy.wait()

    def store(item, c, start):
        length, n, base, held, stays, h = numbers(item)
        ident = head * per_half + c
        j = ident - base
        place = cache.at[item, :, pl.ds(c * CHUNK, CHUNK)]
        sem = sems_out.at[item * 8 + c]

        @pl.when((j >= 0) & (j < held))
        def _():
            copy = pltpu.make_async_copy(keys.at[item, :, lanes(jnp.maximum(j, 0))], place, sem)
            copy.start() if start else copy.wait()

        @pl.when(ident >= n)
        def _():
            copy = pltpu.make_async_copy(zeros, place, sem)
            copy.start() if start else copy.wait()

    for item in range(2):
        for j in range(per_half):
            fetch(item, j, True)

    for item in range(2):
        length, n, base, held, stays, h = numbers(item)
        for step in range(steps):
            queries[pl.ds(step * heads, heads), :] = query[step, item]
            queries[pl.ds(own_rows + step * heads, heads), :] = query_other[step, item]
        new = fresh[item]
        step_of = lax.broadcasted_iota(jnp.int32, (own_rows, new.shape[0]), 0) // heads
        position = lax.broadcasted_iota(jnp.int32, (own_rows, new.shape[0]), 1)
        valid_new = position <= step_of
        new_scores = nt_dot(queries[pl.ds(0, own_rows), :], new) * score_scale
        new_scores = jnp.where(valid_new, new_scores, big_negative)
        top = jnp.concatenate(
            [
                jnp.max(new_scores, axis=1, keepdims=True),
                jnp.full((rows - own_rows, 1), big_negative, jnp.float32),
            ],
            axis=0,
        )
        for j in range(per_half):
            fetch(item, j, False)
        for c in range(per_half):
            store(item, c, True)

        left = length - base * CHUNK

        def score(j, top):
            part = jnp.dot(
                queries[...], keys[item, :, lanes(j)], preferred_element_type=jnp.float32
            )
            where_ = j * CHUNK + lax.broadcasted_iota(jnp.int32, (rows, CHUNK), 1)
            part = jnp.where(where_ < left, part * score_scale, big_negative)
            scores[:, lanes(j)] = part
            return jnp.maximum(top, jnp.max(part, axis=1, keepdims=True))

        top = lax.fori_loop(0, held, score, top)
        own_top = top[:own_rows]
        new_weight = jnp.where(valid_new, jnp.exp(new_scores - own_top), 0.0)
        total[pl.ds(0, own_rows), :] = jnp.dot(
            new_weight.astype(jnp.bfloat16), new[:, :DL], preferred_element_type=jnp.float32
        )
        total[pl.ds(own_rows, rows - own_rows), :] = jnp.zeros(
            (rows - own_rows, DL), jnp.float32
        )
        weight_sum = jnp.concatenate(
            [
                jnp.sum(new_weight, axis=1, keepdims=True),
                jnp.zeros((rows - own_rows, 1), jnp.float32),
            ],
            axis=0,
        )

        def attend(j, weight_sum):
            where_ = j * CHUNK + lax.broadcasted_iota(jnp.int32, (rows, CHUNK), 1)
            weight = jnp.where(where_ < left, jnp.exp(scores[:, lanes(j)] - top), 0.0)
            total[...] += nt_dot(weight.astype(jnp.bfloat16), keys[item, pl.ds(0, DL), lanes(j)])
            return weight_sum + jnp.sum(weight, axis=1, keepdims=True)

        weight_sum = lax.fori_loop(0, held, attend, weight_sum)
        own_sum[item] = total[pl.ds(0, own_rows), :]
        other_sum[item] = total[pl.ds(own_rows, rows - own_rows), :].astype(jnp.bfloat16)
        lane = lax.broadcasted_iota(jnp.int32, (rows, 128), 1)
        stats[item] = jnp.where(lane == 0, top, weight_sum)

    for item in range(2):
        for c in range(per_half):
            store(item, c, False)


def attend(where, plan, query, query_other, fresh, kv, inbox):
    steps, items, heads, width = query.shape
    own = steps * heads
    return pl.pallas_call(
        attend_kernel,
        in_specs=[SMEM, SMEM, VMEM, VMEM, VMEM, ANY, ANY],
        out_specs=[VMEM, VMEM, VMEM, ANY],
        out_shape=[
            jax.ShapeDtypeStruct((items, own, DL), jnp.float32),
            jax.ShapeDtypeStruct((items, own, DL), jnp.bfloat16),
            jax.ShapeDtypeStruct((items, 2 * own, 128), jnp.float32),
            jax.ShapeDtypeStruct(kv.shape, kv.dtype),
        ],
        scratch_shapes=[
            pltpu.VMEM(kv.shape, kv.dtype),
            pltpu.VMEM((2 * own, kv.shape[2]), jnp.float32),
            pltpu.VMEM((2 * own, width), kv.dtype),
            pltpu.VMEM((2 * own, DL), jnp.float32),
            pltpu.VMEM((width, CHUNK), kv.dtype),
            pltpu.SemaphoreType.DMA((16,)),
            pltpu.SemaphoreType.DMA((16,)),
        ],
        compiler_params=pltpu.CompilerParams(vmem_limit_bytes=48 * 2**20),
    )(where, plan, query, query_other, fresh, kv, inbox)


def return_kernel(where, plan, post, _, cache, sems):
    per_half = 2048 // CHUNK
    for start in (True, False):
        for item in range(2):
            at = META + item * N_META
            n, stays, h = plan[at + 1], plan[at + 4], plan[at + 5]
            for q in range(4):

                @pl.when((where[1] == 0) & (stays < 0) & (h + q < jnp.minimum(n, per_half)))
                def _():
                    copy = pltpu.make_async_copy(
                        post.at[item, :, pl.ds(q * CHUNK, CHUNK)],
                        cache.at[item, :, lanes(jnp.minimum(h + q, per_half - 1))],
                        sems.at[item * 4 + q],
                    )
                    copy.start() if start else copy.wait()


def return_rows(where, plan, post, cache):
    return pl.pallas_call(
        return_kernel,
        in_specs=[SMEM, SMEM, VMEM, ANY],
        out_specs=ANY,
        out_shape=jax.ShapeDtypeStruct(cache.shape, cache.dtype),
        input_output_aliases={3: 0},
        scratch_shapes=[pltpu.SemaphoreType.DMA((8,))],
    )(where, plan, post, cache)


def merge_kernel(own_sum, stats, other_sum, other_stats, out):
    items, own, _ = own_sum.shape
    steps, _, heads, _ = out.shape
    for item in range(items):
        one = stats[item, pl.ds(0, own), :]
        two = other_stats[item]
        top = jnp.maximum(one[:, :1], two[:, :1])
        scale_one = jnp.exp(one[:, :1] - top)
        scale_two = jnp.exp(two[:, :1] - top)
        total = one[:, 1:2] * scale_one + two[:, 1:2] * scale_two
        summed = own_sum[item] * scale_one + other_sum[item].astype(jnp.float32) * scale_two
        result = (summed / total).astype(out.dtype)
        for step in range(steps):
            out[step, item] = result[step * heads : (step + 1) * heads]


def merge(own_sum, stats, other_sum, other_stats, steps, heads):
    return pl.pallas_call(
        merge_kernel,
        in_specs=[VMEM] * 4,
        out_specs=VMEM,
        out_shape=jax.ShapeDtypeStruct((steps, own_sum.shape[0], heads, DL), jnp.bfloat16),
    )(own_sum, stats, other_sum, other_stats)


def exchanges(zs):
    even, odd, across = [], [], []
    for z in range(zs):
        for y in range(2):
            across.append((z * 2 + y, z * 2 + 1 - y))
            if z + 1 < zs:
                pairs = even if z % 2 == 0 else odd
                pairs.append((z * 2 + y, z * 2 + 2 + y))
                pairs.append((z * 2 + 2 + y, z * 2 + y))
    return even, odd, across


def routed(zs, kv, lengths, slot_of, query, new_latent):
    kinds = exchanges(zs)
    steps, items, heads, width = query.shape
    where = jnp.stack([lax.axis_index("seq"), lax.axis_index("head")]).astype(jnp.int32)
    kv = jnp.swapaxes(kv, 1, 2)
    swap = [(0, 1), (1, 0)]
    pre = lax.ppermute(hand_over(where, lengths, kv), "head", [(0, 1)])
    query_other = lax.ppermute(query, "head", swap)
    fresh = jnp.pad(jnp.swapaxes(new_latent, 0, 1), ((0, 0), (0, 128 - steps), (0, 0)))
    plan, inbox = make_plan(zs, where, lengths, slot_of, width)

    def step(time, arrived, inbox):
        sends, inbox = one_step(jnp.full((1,), time, jnp.int32), plan, kv, pre, arrived, inbox)
        return [lax.ppermute(s, "seq", k) for s, k in zip(sends, kinds)], inbox

    def run(begin, count, arrived, inbox):
        for k in range(count):
            new, inbox = step(begin + k, arrived[0], inbox)
            arrived = [arrived[1], new]
        return arrived, inbox

    plan, query_other = lax.optimization_barrier((plan, query_other))
    nothing = [jnp.zeros((width, CHUNK), kv.dtype)] * 3
    arrived, inbox = run(0, UNROLLED, [nothing, nothing], inbox)

    last_step = plan[META + 2 * N_META]

    def more(state):
        return state[0] < last_step

    def body(state):
        time, arrived, inbox = state
        arrived, inbox = run(time, BODY, arrived, inbox)
        return time + BODY, arrived, inbox

    time, arrived, inbox = lax.while_loop(more, body, (jnp.int32(UNROLLED), arrived, inbox))
    inbox, post = finish(time[None], plan, arrived[0] + arrived[1], inbox)
    post = lax.ppermute(post, "head", [(1, 0)])
    own_sum, other_sum, stats, cache = attend(
        where, plan, query, query_other, fresh, kv, inbox
    )
    other_sum = lax.ppermute(other_sum, "head", swap)
    other_stats = lax.ppermute(stats[:, steps * heads :], "head", swap)
    cache = return_rows(where, plan, post, cache)
    attended = merge(own_sum, stats, other_sum, other_stats, steps, heads)
    return attended, jnp.swapaxes(cache, 1, 2)


def merged_2(shard, axis, combine):
    everything = jax.tree.map(
        lambda part, kind: lax.all_gather(part.astype(kind), axis),
        shard,
        (jnp.bfloat16, jnp.bfloat16, jnp.bfloat16),
    )

    def take(k):
        return jax.tree.map(lambda part, own: part[k].astype(own.dtype), everything, shard)

    return lax.fori_loop(
        1, lax.axis_size(axis), lambda k, so_far: combine(so_far, take(k)), take(0)
    )


def join_partials(first, second):
    top = jnp.maximum(first[0], second[0])
    scale_one = jnp.exp(first[0] - top)
    scale_two = jnp.exp(second[0] - top)
    total = first[1] * scale_one + second[1] * scale_two
    summed = first[2] * scale_one[..., None] + second[2] * scale_two[..., None]
    return (top, total, summed)


def balanced(kv, lengths, slot_of, query, new_latent):
    req = kv.shape[0]
    half = kv.shape[1]
    count = lengths.shape[0]
    steps_new = query.shape[0]
    heads_here = query.shape[2]
    pieces = lax.all_to_all(kv, "seq", split_axis=1, concat_axis=0, tiled=True)
    inverse = jnp.zeros((count,), jnp.int32).at[slot_of].set(jnp.arange(count, dtype=jnp.int32))
    ordered = jnp.take(pieces, inverse, axis=0)
    cache = lax.all_to_all(ordered, "seq", split_axis=0, concat_axis=1, tiled=True)
    my_lens = lax.dynamic_slice_in_dim(
        jnp.take(lengths, inverse, axis=0), lax.axis_index("seq") * req, req
    )
    head_pos = lax.axis_index("head")
    rows = steps_new * heads_here
    row_step = jnp.arange(rows, dtype=jnp.int32) // heads_here
    valid_two = jnp.arange(steps_new, dtype=jnp.int32)[None, :] <= row_step[:, None]
    results = []
    every_query = lax.all_gather(query, "head", axis=2, tiled=True)
    heads_all = every_query.shape[2]
    rows_all = steps_new * heads_all
    positions = head_pos * half + jnp.arange(half, dtype=jnp.int32)
    tops = []
    totals = []
    sums = []
    for item in range(req):
        queries = every_query[:, item].reshape(rows_all, every_query.shape[3])
        valid_one = positions[None, :] < my_lens[item]
        cache_scores = (
            jnp.einsum("nd,td->nt", queries, cache[item], preferred_element_type=jnp.float32)
            * score_scale
        )
        top = jnp.max(jnp.where(valid_one, cache_scores, big_negative), axis=1)
        weight_one = jnp.where(valid_one, jnp.exp(cache_scores - top[:, None]), 0.0)
        tops.append(top)
        totals.append(jnp.sum(weight_one, axis=1))
        sums.append(
            jnp.dot(
                weight_one.astype(jnp.bfloat16),
                cache[item][:, :DL],
                preferred_element_type=jnp.float32,
            )
        )
    merged = merged_2((jnp.stack(tops), jnp.stack(totals), jnp.stack(sums)), "head", join_partials)
    start = head_pos * heads_here
    own_top = lax.dynamic_slice_in_dim(
        merged[0].reshape(req, steps_new, heads_all), start, heads_here, 2
    ).reshape(req, rows)
    own_total = lax.dynamic_slice_in_dim(
        merged[1].reshape(req, steps_new, heads_all), start, heads_here, 2
    ).reshape(req, rows)
    own_sum = lax.dynamic_slice_in_dim(
        merged[2].reshape(req, steps_new, heads_all, DL), start, heads_here, 2
    ).reshape(req, rows, DL)
    for item in range(req):
        queries = query[:, item].reshape(rows, query.shape[3])
        fresh = new_latent[:, item]
        new_scores = (
            jnp.einsum("nd,td->nt", queries, fresh, preferred_element_type=jnp.float32)
            * score_scale
        )
        top = jnp.maximum(
            own_top[item], jnp.max(jnp.where(valid_two, new_scores, big_negative), axis=1)
        )
        rescale = jnp.exp(own_top[item] - top)
        weight_two = jnp.where(valid_two, jnp.exp(new_scores - top[:, None]), 0.0)
        total = own_total[item] * rescale + jnp.sum(weight_two, axis=1)
        summed = own_sum[item] * rescale[:, None]
        summed = summed + jnp.dot(
            weight_two.astype(jnp.bfloat16), fresh[:, :DL], preferred_element_type=jnp.float32
        )
        results.append(
            (summed / total[:, None]).astype(jnp.bfloat16).reshape(steps_new, heads_here, DL)
        )
    return (jnp.stack(results, axis=1), cache)


def solution(mesh):
    local = functools.partial(routed, 4) if mesh.shape["seq"] == 8 else balanced
    return jax.shard_map(
        local,
        mesh=mesh,
        in_specs=(
            P(("groups", "seq"), "head", None),
            P("groups"),
            P("groups"),
            P(None, ("groups", "seq"), "head", None),
            P(None, ("groups", "seq"), None),
        ),
        out_specs=(P(None, ("groups", "seq"), "head", None), P(("groups", "seq"), "head", None)),
        check_vma=False,
    )
```

```python
import functools

import jax
import jax.numpy as jnp
from jax import lax
from jax.experimental import pallas as pl
from jax.experimental.pallas import tpu as pltpu
from jax.sharding import PartitionSpec as P

DL = 512
CHUNK_BITS = 8
CHUNK = 1 << CHUNK_BITS
LAG = 2
TMAX = 256
UNROLLED = 16
BODY = 3
SLOTS = 160

score_scale = 192.0 ** (-0.5)
big_negative = -1e30

ANY = pl.BlockSpec(memory_space=pl.ANY)
VMEM = pl.BlockSpec(memory_space=pltpu.VMEM)
SMEM = pl.BlockSpec(memory_space=pltpu.SMEM)

SMALL = pltpu.CompilerParams(vmem_limit_bytes=8 * 2**20)

FROM_KV, FROM_PRE, FROM_LINK, FROM_INBOX, NOTHING = 0, 16, 24, 32, 255
OWNED = SLOTS

SEND, KEEP, STAY, LAST, META = 0, TMAX, 2 * TMAX, 2 * TMAX + 16, 2 * TMAX + 32
N_META = 8
PLAN = META + 2 * N_META + 8


def cdiv(a, b):
    return (a + b - 1) // b


def nt_dot(a, b):
    return lax.dot_general(a, b, (((1,), (1,)), ((), ())), preferred_element_type=jnp.float32)


def head_rows(query, item):
    return jnp.concatenate([query[step, item] for step in range(query.shape[0])], axis=0)


def begin_sums(query, fresh, total, stats):
    steps, items, heads, _ = query.shape
    own = steps * heads
    for item in range(items):
        new = fresh[item]
        step_of = lax.broadcasted_iota(jnp.int32, (own, new.shape[0]), 0) // heads
        position = lax.broadcasted_iota(jnp.int32, (own, new.shape[0]), 1)
        valid = position <= step_of
        scores = nt_dot(head_rows(query, item), new) * score_scale
        scores = jnp.where(valid, scores, big_negative)
        top = jnp.max(scores, axis=1, keepdims=True)
        weight = jnp.where(valid, jnp.exp(scores - top), 0.0)
        mine, others = pl.ds(0, own), pl.ds(own, own)
        stats[item, 0, mine, :] = jnp.broadcast_to(top, (own, 128))
        stats[item, 1, mine, :] = jnp.broadcast_to(
            jnp.sum(weight, axis=1, keepdims=True), (own, 128)
        )
        total[item, mine, :] = jnp.dot(
            weight.astype(jnp.bfloat16), new[:, :DL], preferred_element_type=jnp.float32
        )
        stats[item, 0, others, :] = jnp.full((own, 128), big_negative, jnp.float32)
        stats[item, 1, others, :] = jnp.zeros((own, 128), jnp.float32)
        total[item, others, :] = jnp.zeros((own, DL), jnp.float32)


def absorb(plan, item, j, keys, query, query_other, total, stats):
    at = META + item * N_META
    left = plan[at] - (plan[at + 2] + j) * CHUNK

    @pl.when(left > 0)
    def _():
        queries = jnp.concatenate([head_rows(query, item), head_rows(query_other, item)], axis=0)
        scores = jnp.dot(queries, keys[...], preferred_element_type=jnp.float32) * score_scale
        inside = lax.broadcasted_iota(jnp.int32, scores.shape, 1) < left
        scores = jnp.where(inside, scores, big_negative)
        before = stats[item, 0]
        top = jnp.maximum(before, jnp.max(scores, axis=1, keepdims=True))
        scale = jnp.exp(before - top)
        weight = jnp.exp(scores - jnp.concatenate([top] * (CHUNK // 128), axis=1))
        stats[item, 0] = top
        stats[item, 1] = stats[item, 1] * scale + jnp.sum(weight, axis=1, keepdims=True)
        added = nt_dot(weight.astype(jnp.bfloat16), keys[pl.ds(0, DL), :])
        total[item] = total[item] * jnp.concatenate([scale] * (DL // 128), axis=1) + added


def plan_kernel(
    zs, where, lengths, slot_of, query, fresh,
    plan, inbox, cache, post, total, stats,
    busy, load, bucket, var, zeros, sems,
):
    me, head = where[0], where[1]
    words = TMAX // 32
    count = 4 * zs
    per_half = 2048 // CHUNK
    streams = 2 * count

    def fill(ref, begin, size, value):
        wide = 16
        assert size % wide == 0

        def some(i, _):
            for k in range(wide):
                ref[begin + i * wide + k] = value
            return 0

        lax.fori_loop(0, size // wide, some, 0)

    def sizes(r):
        n = (lengths[r] + CHUNK - 1) >> CHUNK_BITS
        return n, (n + 1) >> 1

    fill(plan, 0, 2 * TMAX + 32, jnp.int32(-1))

    var[0] = 0

    def slots(r, _):
        @pl.when(slot_of[r] >> 1 == me)
        def _():
            item = slot_of[r] & 1
            at = META + item * N_META
            n, h = sizes(r)
            stays = r >> 1 == me
            base = jnp.where(head == 0, 0, jnp.where(stays, per_half, h))
            end = jnp.where(
                stays,
                jnp.where(head == 0, jnp.minimum(n, per_half), n),
                jnp.where(head == 0, h, n),
            )
            held = jnp.maximum(end - base, 0)
            plan[at] = lengths[r]
            plan[at + 1] = n
            plan[at + 2] = base
            plan[at + 3] = held
            plan[at + 4] = jnp.where(stays, r & 1, -1)
            plan[at + 5] = h

            def staying(j, _):
                plan[STAY + var[0] + j] = item * 8 + j
                return 0

            staying_here = jnp.where(stays, held, 0)
            lax.fori_loop(0, staying_here, staying, 0)
            var[0] = var[0] + staying_here

        return 0

    lax.fori_loop(0, count, slots, 0)

    zeros[...] = jnp.zeros_like(zeros)

    def blank(start):
        for item in range(2):
            n = plan[META + item * N_META + 1]
            for c in range(per_half):

                @pl.when(head * per_half + c >= n)
                def _():
                    copy = pltpu.make_async_copy(
                        zeros,
                        cache.at[item, :, pl.ds(c * CHUNK, CHUNK)],
                        sems.at[item * per_half + c],
                    )
                    copy.start() if start else copy.wait()

    blank(True)
    begin_sums(query, fresh, total, stats)
    fill(busy, 0, 6 * zs * words, jnp.int32(0))
    for i in range(6 * zs):
        load[i] = 0
    for i in range(zs + 2):
        var[i] = 0
    var[zs + 2] = 0
    var[zs + 3] = 0

    def y_link(z, y):
        return 4 * zs + z * 2 + y

    def route(r, _):
        src = r >> 1
        dst = slot_of[r] >> 1
        n, h = sizes(r)
        z0, y0 = src >> 1, src & 1
        z1, y1 = dst >> 1, dst & 1
        low, high = jnp.minimum(z0, z1), jnp.maximum(z0, z1)
        offset = jnp.where(z1 > z0, 0, 2 * zs)
        inside = [(low <= z) & (z < high) for z in range(zs - 1)]
        turn = jnp.where(y0 == y1, 0, 1)
        for part in range(2):
            amount = jnp.where(src == dst, 0, h >> 1 if part == 0 else h - (h >> 1))

            def cost(col):
                top = jnp.int32(0)
                for z in range(zs - 1):
                    top = jnp.maximum(top, jnp.where(inside[z], load[offset + z * 2 + col], 0))
                return top

            straight = jnp.maximum(cost(y0), jnp.where(turn == 1, load[y_link(z1, y0)], 0))
            other = jnp.maximum(cost(1 - y0), load[y_link(z0, y0)])
            other = jnp.where(
                turn == 1, other, jnp.maximum(other, load[y_link(z1, 1 - y0)])
            )
            col = jnp.where((z0 != z1) & (other < straight), 1 - y0, y0)
            for z in range(zs - 1):
                at = offset + z * 2 + col
                load[at] = load[at] + jnp.where(inside[z], amount, 0)
            first = jnp.where(col != y0, 1, 0)
            last = jnp.where(col != y1, 1, 0)
            at = y_link(z0, y0)
            load[at] = load[at] + first * amount
            at = y_link(z1, col)
            load[at] = load[at] + last * amount
            hops = jnp.where(amount == 0, 0, high - low + first + last)
            filled = var[hops]
            bucket[hops * streams + filled] = r * 4 + part * 2 + col
            var[hops] = filled + 1
        return 0

    lax.fori_loop(0, count, route, 0)

    def stream(hops, index):
        packed = bucket[hops * streams + index]
        r, part, col = packed >> 2, (packed >> 1) & 1, packed & 1
        src = r >> 1
        slot = slot_of[r]
        dst = slot >> 1
        n, h = sizes(r)
        half = h >> 1
        begin = jnp.where(part == 0, 0, half)
        amount = jnp.where(part == 0, half, h - half)
        item = r & 1
        z0, y0 = src >> 1, src & 1
        z1 = dst >> 1
        up = jnp.where(z1 > z0, 1, 0)
        sign = 2 * up - 1
        first = jnp.where(col != y0, 1, 0)
        dz = jnp.abs(z1 - z0)

        def hop(i, state):
            times, kind_before, slot_before = state[:4], state[4], state[5]
            is_first = i < first
            is_last = i >= first + dz
            z = z0 + sign * (i - first)
            edge = z + up - 1
            is_y = is_first | is_last
            z_turn = jnp.where(is_first, z0, z1)
            y_from = jnp.where(is_first, y0, col)
            link = jnp.where(
                is_y, y_link(z_turn, y_from), jnp.where(up == 1, 0, 2 * zs) + edge * 2 + col
            )
            kind = jnp.where(is_y, 2, edge & 1)
            sender = jnp.where(is_y, z_turn, z) * 2 + y_from
            sender = jnp.where(is_y, sender, z * 2 + col)
            receiver = jnp.where(is_y, z_turn * 2 + 1 - y_from, (z + sign) * 2 + col)
            row = link * words
            new_times = []
            for j in range(4):
                start = times[j] + LAG
                word0 = start >> 5
                free0 = ~busy[row + word0] & (jnp.int32(-1) << (start & 31))

                def onward(state):
                    word = state[0] + 1
                    return word, ~busy[row + word]

                word, free = lax.while_loop(lambda s: s[1] == 0, onward, (word0, free0))
                low = jnp.where(j < amount, free & -free, 0)
                busy[row + word] = busy[row + word] | low
                new_times.append(word * 32 + 31 - lax.clz(free & -free))
            slot_now = var[zs + 2]

            @pl.when((sender == me) | (receiver == me))
            def _():
                shift = kind * 8
                for j in range(4):
                    ident = begin + j + jnp.where(head == 0, 0, h)
                    own = FROM_KV + item * per_half + (ident & (per_half - 1))
                    handed = FROM_PRE + item * 4 + ident - jnp.minimum(h, 4)
                    code = jnp.where((head == 1) & (ident < per_half), handed, own)
                    passed = jnp.where(
                        new_times[j] == times[j] + LAG,
                        FROM_LINK + kind_before,
                        FROM_INBOX + slot_before + j,
                    )
                    code = jnp.where(i == 0, code, passed)
                    here = (sender == me) & (j < amount)
                    at = SEND + new_times[j]
                    plan[at] = plan[at] ^ jnp.where(here, (code ^ 255) << shift, 0)
                    here = (receiver == me) & (j < amount)
                    place = jnp.where(
                        dst == me, OWNED + (slot & 1) * 8 + begin + j, slot_now + j
                    )
                    at = KEEP + new_times[j] + LAG
                    plan[at] = plan[at] ^ jnp.where(here, (place ^ 255) << shift, 0)
                    at = jnp.where(here & (dst == me), LAST + place - OWNED, PLAN - 1)
                    plan[at] = new_times[j] + LAG
                kept = (receiver == me) & (dst != me)
                var[zs + 2] = slot_now + jnp.where(kept, amount, 0)

            return (*new_times, kind, slot_now)

        early = jnp.int32(-LAG)
        state = lax.fori_loop(0, hops, hop, (early, early, early, early, jnp.int32(0), jnp.int32(0)))
        end = jnp.maximum(jnp.maximum(state[0], state[1]), jnp.maximum(state[2], state[3]))
        for j in range(4):
            end = jnp.where(j == amount - 1, state[j], end)
        var[zs + 3] = jnp.maximum(var[zs + 3], end + 1)

    def by_hops(k, _):
        hops = zs + 1 - k

        def each(index, _):
            stream(hops, index)
            return 0

        lax.fori_loop(0, var[hops], each, 0)
        return 0

    lax.fori_loop(0, zs + 1, by_hops, 0)

    plan[META + 2 * N_META] = var[zs + 3]
    blank(False)


def make_plan(zs, where, lengths, slot_of, query, fresh, kv):
    steps, items, heads, width = query.shape
    rows = 2 * steps * heads
    return pl.pallas_call(
        functools.partial(plan_kernel, zs),
        in_specs=[SMEM] * 3 + [VMEM] * 2,
        out_specs=[SMEM] + [ANY] * 3 + [VMEM] * 2,
        out_shape=[
            jax.ShapeDtypeStruct((PLAN,), jnp.int32),
            pltpu.HBM((SLOTS + 16, width, CHUNK), kv.dtype),
            pltpu.HBM(kv.shape, kv.dtype),
            pltpu.HBM((items, width, 4 * CHUNK), kv.dtype),
            pltpu.VMEM((items, rows, DL), jnp.float32),
            pltpu.VMEM((items, 2, rows, 128), jnp.float32),
        ],
        scratch_shapes=[
            pltpu.SMEM((6 * zs * (TMAX // 32),), jnp.int32),
            pltpu.SMEM((6 * zs,), jnp.int32),
            pltpu.SMEM(((zs + 2) * 8 * zs,), jnp.int32),
            pltpu.SMEM((zs + 4,), jnp.int32),
            pltpu.VMEM((width, CHUNK), kv.dtype),
            pltpu.SemaphoreType.DMA((16,)),
        ],
        compiler_params=SMALL,
    )(where, lengths, slot_of, query, fresh)


def lanes(index):
    return pl.ds(pl.multiple_of(index * CHUNK, CHUNK), CHUNK)


def hand_kernel(where, lengths, kv, out, sems):
    for start in (True, False):
        for item in range(2):
            n = cdiv(lengths[where[0] * 2 + item], CHUNK)
            first = jnp.minimum(cdiv(n, 2), 4)
            for q in range(4):
                copy = pltpu.make_async_copy(
                    kv.at[item, :, lanes(first + q)],
                    out.at[item, :, pl.ds(q * CHUNK, CHUNK)],
                    sems.at[item * 4 + q],
                )
                if start:
                    copy.start()
                else:
                    copy.wait()


def hand_over(where, lengths, kv):
    return pl.pallas_call(
        hand_kernel,
        in_specs=[SMEM, SMEM, ANY],
        out_specs=VMEM,
        out_shape=pltpu.VMEM((2, kv.shape[1], 4 * CHUNK), kv.dtype),
        scratch_shapes=[pltpu.SemaphoreType.DMA((8,))],
        compiler_params=SMALL,
    )(where, lengths, kv)


def owned_chunk(plan, code):
    item, j = (code >> 3) & 1, code & 7
    at = META + item * N_META
    ident = plan[at + 2] + j
    return item, j, ident, ident < plan[at + 1]


def store_owned(plan, head, code, rows, cache, post, sem, start):
    item, j, ident, real = owned_chunk(plan, code)
    per_half = 2048 // CHUNK
    here = ident >> 3 == head

    @pl.when(real & here)
    def _():
        copy = pltpu.make_async_copy(rows, cache.at[item, :, lanes(ident & (per_half - 1))], sem)
        copy.start() if start else copy.wait()

    @pl.when(real & ~here)
    def _():
        copy = pltpu.make_async_copy(rows, post.at[item, :, lanes(j & 3)], sem)
        copy.start() if start else copy.wait()


def step_kernel(taking, time, where, plan, kv, pre, *refs):
    if taking:
        query, query_other, *refs = refs
        arrived, refs = refs[:3], refs[8:]
        sends, inbox, (cache, post, total, stats, local, sems) = refs[:3], refs[3], refs[4:]
    else:
        arrived, refs = refs[:3], refs[4:]
        sends, (inbox, sems) = refs[:3], refs[3:]
    head = where[1]
    to_send, to_keep = plan[SEND + time[0]], plan[KEEP + time[0]]
    codes = [(to_send >> (8 * kind)) & 255 for kind in range(3)]
    places = [(to_keep >> (8 * kind)) & 255 for kind in range(3)]
    waiting = OWNED if taking else NOTHING

    def load_from(source, kind):
        return pltpu.make_async_copy(source, sends[kind], sems.at[kind])

    def keep(kind):
        place = jnp.minimum(places[kind], SLOTS + 15)
        return pltpu.make_async_copy(arrived[kind], inbox.at[place], sems.at[3 + kind])

    for kind in range(3):
        code = codes[kind]

        @pl.when(code < FROM_PRE)
        def _():
            load_from(kv.at[code >> 3, :, lanes(code & 7)], kind).start()

        @pl.when((code >= FROM_PRE) & (code < FROM_LINK))
        def _():
            load_from(pre.at[(code - FROM_PRE) >> 2, :, lanes(code & 3)], kind).start()

        for other in range(3):

            @pl.when(code == FROM_LINK + other)
            def _():
                load_from(arrived[other], kind).start()

        @pl.when((code >= FROM_INBOX) & (code < NOTHING))
        def _():
            load_from(inbox.at[code - FROM_INBOX], kind).start()

        @pl.when(places[kind] < waiting)
        def _():
            keep(kind).start()

    if taking:
        staying = plan[STAY + time[0]]

        def load_local():
            item = (staying >> 3) & 1
            source = jnp.maximum(plan[META + item * N_META + 4], 0)
            return pltpu.make_async_copy(kv.at[source, :, lanes(staying & 7)], local, sems.at[6])

        @pl.when(staying >= 0)
        def _():
            load_local().start()

        def take(code, rows, sem):
            store_owned(plan, head, code, rows, cache, post, sem, True)
            item, j, _, _ = owned_chunk(plan, code)
            absorb(plan, item, j, rows, query, query_other, total, stats)

        for kind in range(3):

            @pl.when((places[kind] >= OWNED) & (places[kind] < NOTHING))
            def _():
                take(places[kind] - OWNED, arrived[kind], sems.at[3 + kind])

        @pl.when(staying >= 0)
        def _():
            load_local().wait()
            take(staying, local, sems.at[7])
            store_owned(plan, head, staying, local, cache, post, sems.at[7], False)

    for kind in range(3):

        @pl.when(codes[kind] < NOTHING)
        def _():
            load_from(arrived[kind], kind).wait()

        @pl.when(places[kind] < waiting)
        def _():
            keep(kind).wait()

        if taking:

            @pl.when((places[kind] >= OWNED) & (places[kind] < NOTHING))
            def _():
                code = places[kind] - OWNED
                store_owned(plan, head, code, arrived[kind], cache, post, sems.at[3 + kind], False)


def in_hbm(arrays):
    return [pltpu.with_memory_space_constraint(a, pltpu.HBM) for a in arrays]


def in_vmem(arrays):
    return [pltpu.with_memory_space_constraint(a, pltpu.VMEM) for a in arrays]


def like(state):
    shapes = [pltpu.HBM(a.shape, a.dtype) for a in state[:3]]
    return shapes + [pltpu.VMEM(a.shape, a.dtype) for a in state[3:]]


def one_step(taking, time, where, plan, kv, pre, queries, arrived, state):
    inbox = state[0]
    piece = pltpu.VMEM(inbox.shape[1:], inbox.dtype)
    queries = queries if taking else ()
    state = state if taking else state[:1]
    first = 5 + len(queries) + 3
    wide = [ANY] * 3 + [VMEM] * 2 if taking else [ANY]
    scratch = [pltpu.VMEM(inbox.shape[1:], inbox.dtype)] if taking else []
    out = pl.pallas_call(
        functools.partial(step_kernel, taking),
        in_specs=[SMEM] * 3 + [ANY] * 2 + [VMEM] * (len(queries) + 3) + wide,
        out_specs=[VMEM] * 3 + wide,
        out_shape=[piece] * 3 + like(state),
        input_output_aliases={first + k: 3 + k for k in range(len(state))},
        scratch_shapes=scratch + [pltpu.SemaphoreType.DMA((8,))],
        compiler_params=SMALL,
        cost_estimate=pl.CostEstimate(
            flops=0, bytes_accessed=12 * inbox.shape[1] * CHUNK, transcendentals=0
        ),
    )(
        time, where, plan, *in_hbm([kv, pre]), *in_vmem([*queries, *arrived]),
        *in_hbm(state[:3]), *in_vmem(state[3:]),
    )
    return out[:3], out[3:]


def finish_kernel(time, where, plan, query, query_other, inbox, *refs):
    arrived, refs = refs[: 3 * LAG], refs[3 * LAG + 4 :]
    cache, post, total, stats, other_sum, other_stats, local, sems = refs
    head = where[1]
    own = other_sum.shape[1]

    def take_waiting(code, _):
        row = plan[LAST + code]

        @pl.when((row >= UNROLLED) & (row < time[0]))
        def _():
            load = pltpu.make_async_copy(inbox.at[OWNED + code], local, sems.at[3 * LAG])
            load.start()
            load.wait()
            store_owned(plan, head, code, local, cache, post, sems.at[3 * LAG], True)
            item, j, _, _ = owned_chunk(plan, code)
            absorb(plan, item, j, local, query, query_other, total, stats)
            store_owned(plan, head, code, local, cache, post, sems.at[3 * LAG], False)

        return 0

    @pl.when(time[0] > UNROLLED)
    def _():
        lax.fori_loop(0, 16, take_waiting, 0)

    for start in (True, False):
        for late in range(LAG):
            word = plan[KEEP + time[0] + late]
            for kind in range(3):
                place = (word >> (8 * kind)) & 255
                rows = arrived[3 * late + kind]
                code = place - OWNED

                @pl.when((place >= OWNED) & (place < NOTHING))
                def _():
                    sem = sems.at[3 * late + kind]
                    store_owned(plan, head, code, rows, cache, post, sem, start)
                    if start:
                        item, j, _, _ = owned_chunk(plan, code)
                        absorb(plan, item, j, rows, query, query_other, total, stats)

    for item in range(other_sum.shape[0]):
        others = pl.ds(own, own)
        other_sum[item] = total[item, others, :].astype(other_sum.dtype)
        lane = lax.broadcasted_iota(jnp.int32, (own, 128), 1)
        other_stats[item] = jnp.where(
            lane == 0, stats[item, 0, others, :], stats[item, 1, others, :]
        )


def finish(time, where, plan, query, query_other, arrived, state):
    items, rows, width = state[3].shape
    shapes = like(state)[1:]
    return pl.pallas_call(
        finish_kernel,
        in_specs=[SMEM] * 3 + [VMEM] * 2 + [ANY] + [VMEM] * (3 * LAG) + [ANY] * 2 + [VMEM] * 2,
        out_specs=[ANY] * 2 + [VMEM] * 4,
        out_shape=shapes
        + [
            pltpu.VMEM((items, rows // 2, width), jnp.bfloat16),
            pltpu.VMEM((items, rows // 2, 128), jnp.float32),
        ],
        input_output_aliases={6 + 3 * LAG + k: k for k in range(4)},
        scratch_shapes=[
            pltpu.VMEM(state[0].shape[1:], state[0].dtype),
            pltpu.SemaphoreType.DMA((3 * LAG + 1,)),
        ],
        compiler_params=SMALL,
    )(
        time, where, plan, *in_vmem([query, query_other]), *in_hbm(state[:1]), *in_vmem(arrived),
        *in_hbm(state[1:3]), *in_vmem(state[3:]),
    )


def return_kernel(where, plan, post, _, cache, sems):
    per_half = 2048 // CHUNK
    for start in (True, False):
        for item in range(2):
            at = META + item * N_META
            n, stays, h = plan[at + 1], plan[at + 4], plan[at + 5]
            for q in range(4):

                @pl.when((where[1] == 0) & (stays < 0) & (h + q < jnp.minimum(n, per_half)))
                def _():
                    copy = pltpu.make_async_copy(
                        post.at[item, :, pl.ds(q * CHUNK, CHUNK)],
                        cache.at[item, :, lanes(jnp.minimum(h + q, per_half - 1))],
                        sems.at[item * 4 + q],
                    )
                    copy.start() if start else copy.wait()


def return_rows(where, plan, post, cache):
    return pl.pallas_call(
        return_kernel,
        in_specs=[SMEM, SMEM, VMEM, ANY],
        out_specs=ANY,
        out_shape=jax.ShapeDtypeStruct(cache.shape, cache.dtype),
        input_output_aliases={3: 0},
        scratch_shapes=[pltpu.SemaphoreType.DMA((8,))],
    )(where, plan, post, *in_hbm([cache]))


def merge_kernel(total, stats, other_sum, other_stats, out):
    items, own, _ = other_sum.shape
    steps, _, heads, _ = out.shape
    mine = pl.ds(0, own)
    for item in range(items):
        top_one, sum_one = stats[item, 0, mine, :][:, :1], stats[item, 1, mine, :][:, :1]
        top_two, sum_two = other_stats[item][:, :1], other_stats[item][:, 1:2]
        top = jnp.maximum(top_one, top_two)
        scale_one = jnp.exp(top_one - top)
        scale_two = jnp.exp(top_two - top)
        weight_sum = sum_one * scale_one + sum_two * scale_two
        summed = total[item, mine, :] * scale_one
        summed = summed + other_sum[item].astype(jnp.float32) * scale_two
        result = (summed / weight_sum).astype(out.dtype)
        for step in range(steps):
            out[step, item] = result[step * heads : (step + 1) * heads]


def merge(total, stats, other_sum, other_stats, steps, heads):
    return pl.pallas_call(
        merge_kernel,
        in_specs=[VMEM] * 4,
        out_specs=VMEM,
        out_shape=jax.ShapeDtypeStruct((steps, total.shape[0], heads, DL), jnp.bfloat16),
        compiler_params=SMALL,
    )(*in_vmem([total, stats, other_sum, other_stats]))


def exchanges(zs):
    even, odd, across = [], [], []
    for z in range(zs):
        for y in range(2):
            across.append((z * 2 + y, z * 2 + 1 - y))
            if z + 1 < zs:
                pairs = even if z % 2 == 0 else odd
                pairs.append((z * 2 + y, z * 2 + 2 + y))
                pairs.append((z * 2 + 2 + y, z * 2 + y))
    return even, odd, across


def routed(zs, kv, lengths, slot_of, query, new_latent):
    kinds = exchanges(zs)
    steps, items, heads, width = query.shape
    where = jnp.stack([lax.axis_index("seq"), lax.axis_index("head")]).astype(jnp.int32)
    kv = jnp.swapaxes(kv, 1, 2)
    swap = [(0, 1), (1, 0)]
    pre = lax.ppermute(hand_over(where, lengths, kv), "head", [(0, 1)])
    query_other = lax.ppermute(query, "head", swap)
    fresh = jnp.pad(jnp.swapaxes(new_latent, 0, 1), ((0, 0), (0, 128 - steps), (0, 0)))
    plan, *state = make_plan(zs, where, lengths, slot_of, query, fresh, kv)
    plan, query_other = lax.optimization_barrier((plan, query_other))

    def run(taking, begin, count, arrived, state):
        for k in range(count):
            time = jnp.full((1,), begin + k, jnp.int32)
            queries = (query, query_other)
            sends, state = one_step(
                taking, time, where, plan, kv, pre, queries, arrived[0], state
            )
            new = [lax.ppermute(s, "seq", pairs) for s, pairs in zip(sends, kinds)]
            arrived = arrived[1:] + [new]
        return arrived, state

    nothing = [jnp.zeros((width, CHUNK), kv.dtype)] * 3
    arrived, state = run(True, 0, UNROLLED, [nothing] * LAG, state)
    last_step = plan[META + 2 * N_META]

    def more(carry):
        return carry[0] < last_step

    def body(carry):
        time, arrived, inbox = carry
        arrived, (inbox,) = run(False, time, BODY, arrived, [inbox])
        return time + BODY, arrived, inbox

    inbox, *state = state
    time, arrived, inbox = lax.while_loop(more, body, (jnp.int32(UNROLLED), arrived, inbox))
    cache, post, total, stats, other_sum, other_stats = finish(
        time[None], where, plan, query, query_other, sum(arrived, []), [inbox, *state]
    )
    post = lax.ppermute(post, "head", [(1, 0)])
    other_sum = lax.ppermute(other_sum, "head", swap)
    other_stats = lax.ppermute(other_stats, "head", swap)
    attended = merge(total, stats, other_sum, other_stats, steps, heads)
    cache = return_rows(where, plan, post, cache)
    return attended, jnp.swapaxes(cache, 1, 2)


def merged_2(shard, axis, combine):
    everything = jax.tree.map(
        lambda part, kind: lax.all_gather(part.astype(kind), axis),
        shard,
        (jnp.bfloat16, jnp.bfloat16, jnp.bfloat16),
    )

    def take(k):
        return jax.tree.map(lambda part, own: part[k].astype(own.dtype), everything, shard)

    return lax.fori_loop(
        1, lax.axis_size(axis), lambda k, so_far: combine(so_far, take(k)), take(0)
    )


def join_partials(first, second):
    top = jnp.maximum(first[0], second[0])
    scale_one = jnp.exp(first[0] - top)
    scale_two = jnp.exp(second[0] - top)
    total = first[1] * scale_one + second[1] * scale_two
    summed = first[2] * scale_one[..., None] + second[2] * scale_two[..., None]
    return (top, total, summed)


def balanced(kv, lengths, slot_of, query, new_latent):
    req = kv.shape[0]
    half = kv.shape[1]
    count = lengths.shape[0]
    steps_new = query.shape[0]
    heads_here = query.shape[2]
    pieces = lax.all_to_all(kv, "seq", split_axis=1, concat_axis=0, tiled=True)
    inverse = jnp.zeros((count,), jnp.int32).at[slot_of].set(jnp.arange(count, dtype=jnp.int32))
    ordered = jnp.take(pieces, inverse, axis=0)
    cache = lax.all_to_all(ordered, "seq", split_axis=0, concat_axis=1, tiled=True)
    my_lens = lax.dynamic_slice_in_dim(
        jnp.take(lengths, inverse, axis=0), lax.axis_index("seq") * req, req
    )
    head_pos = lax.axis_index("head")
    rows = steps_new * heads_here
    row_step = jnp.arange(rows, dtype=jnp.int32) // heads_here
    valid_two = jnp.arange(steps_new, dtype=jnp.int32)[None, :] <= row_step[:, None]
    results = []
    every_query = lax.all_gather(query, "head", axis=2, tiled=True)
    heads_all = every_query.shape[2]
    rows_all = steps_new * heads_all
    positions = head_pos * half + jnp.arange(half, dtype=jnp.int32)
    tops = []
    totals = []
    sums = []
    for item in range(req):
        queries = every_query[:, item].reshape(rows_all, every_query.shape[3])
        valid_one = positions[None, :] < my_lens[item]
        cache_scores = (
            jnp.einsum("nd,td->nt", queries, cache[item], preferred_element_type=jnp.float32)
            * score_scale
        )
        top = jnp.max(jnp.where(valid_one, cache_scores, big_negative), axis=1)
        weight_one = jnp.where(valid_one, jnp.exp(cache_scores - top[:, None]), 0.0)
        tops.append(top)
        totals.append(jnp.sum(weight_one, axis=1))
        sums.append(
            jnp.dot(
                weight_one.astype(jnp.bfloat16),
                cache[item][:, :DL],
                preferred_element_type=jnp.float32,
            )
        )
    merged = merged_2((jnp.stack(tops), jnp.stack(totals), jnp.stack(sums)), "head", join_partials)
    start = head_pos * heads_here
    own_top = lax.dynamic_slice_in_dim(
        merged[0].reshape(req, steps_new, heads_all), start, heads_here, 2
    ).reshape(req, rows)
    own_total = lax.dynamic_slice_in_dim(
        merged[1].reshape(req, steps_new, heads_all), start, heads_here, 2
    ).reshape(req, rows)
    own_sum = lax.dynamic_slice_in_dim(
        merged[2].reshape(req, steps_new, heads_all, DL), start, heads_here, 2
    ).reshape(req, rows, DL)
    for item in range(req):
        queries = query[:, item].reshape(rows, query.shape[3])
        fresh = new_latent[:, item]
        new_scores = (
            jnp.einsum("nd,td->nt", queries, fresh, preferred_element_type=jnp.float32)
            * score_scale
        )
        top = jnp.maximum(
            own_top[item], jnp.max(jnp.where(valid_two, new_scores, big_negative), axis=1)
        )
        rescale = jnp.exp(own_top[item] - top)
        weight_two = jnp.where(valid_two, jnp.exp(new_scores - top[:, None]), 0.0)
        total = own_total[item] * rescale + jnp.sum(weight_two, axis=1)
        summed = own_sum[item] * rescale[:, None]
        summed = summed + jnp.dot(
            weight_two.astype(jnp.bfloat16), fresh[:, :DL], preferred_element_type=jnp.float32
        )
        results.append(
            (summed / total[:, None]).astype(jnp.bfloat16).reshape(steps_new, heads_here, DL)
        )
    return (jnp.stack(results, axis=1), cache)


def solution(mesh):
    local = functools.partial(routed, 4) if mesh.shape["seq"] == 8 else balanced
    return jax.shard_map(
        local,
        mesh=mesh,
        in_specs=(
            P(("groups", "seq"), "head", None),
            P("groups"),
            P("groups"),
            P(None, ("groups", "seq"), "head", None),
            P(None, ("groups", "seq"), None),
        ),
        out_specs=(P(None, ("groups", "seq"), "head", None), P(("groups", "seq"), "head", None)),
        check_vma=False,
    )
```

```python
import functools

import jax
import jax.numpy as jnp
from jax import lax
from jax.experimental import pallas as pl
from jax.experimental.pallas import tpu as pltpu
from jax.sharding import PartitionSpec as P

DL = 512
CHUNK_BITS = 8
CHUNK = 1 << CHUNK_BITS
LAG = 2
TMAX = 256
UNROLLED = 16
BODY = 3
SLOTS = 160

score_scale = 192.0 ** (-0.5)
big_negative = -1e30

ANY = pl.BlockSpec(memory_space=pl.ANY)
VMEM = pl.BlockSpec(memory_space=pltpu.VMEM)
SMEM = pl.BlockSpec(memory_space=pltpu.SMEM)

SMALL = pltpu.CompilerParams(vmem_limit_bytes=8 * 2**20)

FROM_KV, FROM_PRE, FROM_LINK, FROM_INBOX, NOTHING = 0, 16, 24, 32, 255
OWNED = SLOTS

SEND, KEEP, STAY, LAST, META = 0, TMAX, 2 * TMAX, 2 * TMAX + 16, 2 * TMAX + 32
N_META = 8
PLAN = META + 2 * N_META + 8


def cdiv(a, b):
    return (a + b - 1) // b


def nt_dot(a, b):
    return lax.dot_general(a, b, (((1,), (1,)), ((), ())), preferred_element_type=jnp.float32)


def head_rows(query, item):
    return jnp.concatenate([query[step, item] for step in range(query.shape[0])], axis=0)


def begin_sums(query, fresh, total, stats):
    steps, items, heads, _ = query.shape
    own = steps * heads
    for item in range(items):
        new = fresh[item]
        step_of = lax.broadcasted_iota(jnp.int32, (own, new.shape[0]), 0) // heads
        position = lax.broadcasted_iota(jnp.int32, (own, new.shape[0]), 1)
        valid = position <= step_of
        scores = nt_dot(head_rows(query, item), new) * score_scale
        scores = jnp.where(valid, scores, big_negative)
        top = jnp.max(scores, axis=1, keepdims=True)
        weight = jnp.where(valid, jnp.exp(scores - top), 0.0)
        mine, others = pl.ds(0, own), pl.ds(own, own)
        stats[item, 0, mine, :] = jnp.broadcast_to(top, (own, 128))
        stats[item, 1, mine, :] = jnp.broadcast_to(
            jnp.sum(weight, axis=1, keepdims=True), (own, 128)
        )
        total[item, mine, :] = jnp.dot(
            weight.astype(jnp.bfloat16), new[:, :DL], preferred_element_type=jnp.float32
        )
        stats[item, 0, others, :] = jnp.full((own, 128), big_negative, jnp.float32)
        stats[item, 1, others, :] = jnp.zeros((own, 128), jnp.float32)
        total[item, others, :] = jnp.zeros((own, DL), jnp.float32)


def absorb(plan, item, j, keys, query, query_other, total, stats):
    at = META + item * N_META
    left = plan[at] - (plan[at + 2] + j) * CHUNK

    @pl.when(left > 0)
    def _():
        queries = jnp.concatenate([head_rows(query, item), head_rows(query_other, item)], axis=0)
        scores = jnp.dot(queries, keys[...], preferred_element_type=jnp.float32) * score_scale
        inside = lax.broadcasted_iota(jnp.int32, scores.shape, 1) < left
        scores = jnp.where(inside, scores, big_negative)
        before = stats[item, 0]
        top = jnp.maximum(before, jnp.max(scores, axis=1, keepdims=True))
        scale = jnp.exp(before - top)
        weight = jnp.exp(scores - jnp.concatenate([top] * (CHUNK // 128), axis=1))
        stats[item, 0] = top
        stats[item, 1] = stats[item, 1] * scale + jnp.sum(weight, axis=1, keepdims=True)
        added = nt_dot(weight.astype(jnp.bfloat16), keys[pl.ds(0, DL), :])
        total[item] = total[item] * jnp.concatenate([scale] * (DL // 128), axis=1) + added


def plan_kernel(
    zs, where, lengths, slot_of, query, fresh,
    plan, inbox, cache, post, total, stats,
    busy, load, bucket, by_size, var, zeros, sems,
):
    me, head = where[0], where[1]
    words = TMAX // 32 + 1
    count = 4 * zs
    per_half = 2048 // CHUNK
    streams = 2 * count

    def fill(ref, begin, size, value):
        wide = 8
        assert size % wide == 0

        def some(i, _):
            for k in range(wide):
                ref[begin + i * wide + k] = value
            return 0

        lax.fori_loop(0, size // wide, some, 0)

    def sizes(r):
        n = (lengths[r] + CHUNK - 1) >> CHUNK_BITS
        return n, (n + 1) >> 1

    fill(plan, 0, 2 * TMAX + 32, jnp.int32(-1))

    var[0] = 0

    def slots(r, _):
        @pl.when(slot_of[r] >> 1 == me)
        def _():
            item = slot_of[r] & 1
            at = META + item * N_META
            n, h = sizes(r)
            stays = r >> 1 == me
            base = jnp.where(head == 0, 0, jnp.where(stays, per_half, h))
            end = jnp.where(
                stays,
                jnp.where(head == 0, jnp.minimum(n, per_half), n),
                jnp.where(head == 0, h, n),
            )
            held = jnp.maximum(end - base, 0)
            plan[at] = lengths[r]
            plan[at + 1] = n
            plan[at + 2] = base
            plan[at + 3] = held
            plan[at + 4] = jnp.where(stays, r & 1, -1)
            plan[at + 5] = h

            def staying(j, _):
                plan[STAY + var[0] + j] = item * 8 + j
                return 0

            staying_here = jnp.where(stays, held, 0)
            lax.fori_loop(0, staying_here, staying, 0)
            var[0] = var[0] + staying_here

        return 0

    lax.fori_loop(0, count, slots, 0)

    zeros[...] = jnp.zeros_like(zeros)

    def blank(start):
        for item in range(2):
            n = plan[META + item * N_META + 1]
            for c in range(per_half):

                @pl.when(head * per_half + c >= n)
                def _():
                    copy = pltpu.make_async_copy(
                        zeros,
                        cache.at[item, :, pl.ds(c * CHUNK, CHUNK)],
                        sems.at[item * per_half + c],
                    )
                    copy.start() if start else copy.wait()

    blank(True)
    begin_sums(query, fresh, total, stats)
    fill(busy, 0, 6 * zs * words, jnp.int32(0))
    for i in range(6 * zs):
        load[i] = 0
    for i in range(zs + 2):
        var[i] = 0
    var[zs + 2] = 0
    var[zs + 3] = 0

    def y_link(z, y):
        return 4 * zs + z * 2 + y

    for i in range(9):
        var[zs + 4 + i] = 0

    def sort(r, _):
        h = sizes(r)[1]
        filled = var[zs + 4 + h]
        by_size[h * count + filled] = r
        var[zs + 4 + h] = filled + 1
        return 0

    lax.fori_loop(0, count, sort, 0)

    def route(r):
        src = r >> 1
        dst = slot_of[r] >> 1
        n, h = sizes(r)
        z0, y0 = src >> 1, src & 1
        z1, y1 = dst >> 1, dst & 1
        low, high = jnp.minimum(z0, z1), jnp.maximum(z0, z1)
        offset = jnp.where(z1 > z0, 0, 2 * zs)
        inside = [(low <= z) & (z < high) for z in range(zs - 1)]
        turn = jnp.where(y0 == y1, 0, 1)
        for part in range(2):
            amount = jnp.where(src == dst, 0, h >> 1 if part == 0 else h - (h >> 1))

            def cost(col):
                top = jnp.int32(0)
                for z in range(zs - 1):
                    top = jnp.maximum(top, jnp.where(inside[z], load[offset + z * 2 + col], 0))
                return top

            straight = jnp.maximum(cost(y0), jnp.where(turn == 1, load[y_link(z1, y0)], 0))
            other = jnp.maximum(cost(1 - y0), load[y_link(z0, y0)])
            other = jnp.where(
                turn == 1, other, jnp.maximum(other, load[y_link(z1, 1 - y0)])
            )
            col = jnp.where((z0 != z1) & (other < straight), 1 - y0, y0)
            for z in range(zs - 1):
                at = offset + z * 2 + col
                load[at] = load[at] + jnp.where(inside[z], amount, 0)
            first = jnp.where(col != y0, 1, 0)
            last = jnp.where(col != y1, 1, 0)
            at = y_link(z0, y0)
            load[at] = load[at] + first * amount
            at = y_link(z1, col)
            load[at] = load[at] + last * amount
            hops = jnp.where(amount == 0, 0, high - low + first + last)
            filled = var[hops]
            bucket[hops * streams + filled] = r * 4 + part * 2 + col
            var[hops] = filled + 1

    def routes(k, _):
        h = per_half - k

        def each(index, _):
            route(by_size[h * count + index])
            return 0

        lax.fori_loop(0, var[zs + 4 + h], each, 0)
        return 0

    lax.fori_loop(0, per_half, routes, 0)

    def stream(hops, index):
        packed = bucket[hops * streams + index]
        r, part, col = packed >> 2, (packed >> 1) & 1, packed & 1
        src = r >> 1
        slot = slot_of[r]
        dst = slot >> 1
        n, h = sizes(r)
        half = h >> 1
        begin = jnp.where(part == 0, 0, half)
        amount = jnp.where(part == 0, half, h - half)
        item = r & 1
        z0, y0 = src >> 1, src & 1
        z1 = dst >> 1
        up = jnp.where(z1 > z0, 1, 0)
        sign = 2 * up - 1
        first = jnp.where(col != y0, 1, 0)
        dz = jnp.abs(z1 - z0)

        def hop(i, state):
            times, kind_before, slot_before = state[:4], state[4], state[5]
            is_first = i < first
            is_last = i >= first + dz
            z = z0 + sign * (i - first)
            edge = z + up - 1
            is_y = is_first | is_last
            z_turn = jnp.where(is_first, z0, z1)
            y_from = jnp.where(is_first, y0, col)
            link = jnp.where(
                is_y, y_link(z_turn, y_from), jnp.where(up == 1, 0, 2 * zs) + edge * 2 + col
            )
            kind = jnp.where(is_y, 2, edge & 1)
            sender = jnp.where(is_y, z_turn, z) * 2 + y_from
            sender = jnp.where(is_y, sender, z * 2 + col)
            receiver = jnp.where(is_y, z_turn * 2 + 1 - y_from, (z + sign) * 2 + col)
            row = link * words

            start = times[0] + LAG
            word, shift = start >> 5, start & 31
            low_word, high_word = busy[row + word], busy[row + word + 1]
            free = ~(lax.shift_right_logical(low_word, shift) | ((high_word << 1) << (31 - shift)))
            used, fits, quick = jnp.int32(0), jnp.bool_(True), []
            for j in range(4):
                placed = j < amount
                wait = times[j] - times[0]
                allowed = free & (jnp.int32(-1) << jnp.minimum(wait, 31))
                lowest = allowed & -allowed
                fits = fits & ((placed & (allowed != 0) & (wait < 32)) | ~placed)
                lowest = jnp.where(placed, lowest, 0)
                free = free & ~lowest
                used = used | lowest
                time = start + 31 - lax.clz(lowest)
                quick.append(time if j == 0 else jnp.where(placed, time, quick[-1]))

            def in_window():
                busy[row + word] = low_word | (used << shift)
                busy[row + word + 1] = high_word | lax.shift_right_logical(
                    lax.shift_right_logical(used, 1), 31 - shift
                )
                return tuple(quick)

            def beyond():
                found = []
                for j in range(4):
                    begin_at = times[j] + LAG
                    word0 = begin_at >> 5
                    free0 = ~busy[row + word0] & (jnp.int32(-1) << (begin_at & 31))

                    def onward(state):
                        word = state[0] + 1
                        return word, ~busy[row + word]

                    at, free = lax.while_loop(lambda s: s[1] == 0, onward, (word0, free0))
                    lowest = free & -free
                    busy[row + at] = busy[row + at] | jnp.where(j < amount, lowest, 0)
                    time = at * 32 + 31 - lax.clz(lowest)
                    found.append(time if j == 0 else jnp.where(j < amount, time, found[-1]))
                return tuple(found)

            new_times = lax.cond(fits, in_window, beyond)
            slot_now = var[zs + 2]

            @pl.when((sender == me) | (receiver == me))
            def _():
                shift = kind * 8
                for j in range(4):
                    ident = begin + j + jnp.where(head == 0, 0, h)
                    own = FROM_KV + item * per_half + (ident & (per_half - 1))
                    handed = FROM_PRE + item * 4 + ident - jnp.minimum(h, 4)
                    code = jnp.where((head == 1) & (ident < per_half), handed, own)
                    passed = jnp.where(
                        new_times[j] == times[j] + LAG,
                        FROM_LINK + kind_before,
                        FROM_INBOX + slot_before + j,
                    )
                    code = jnp.where(i == 0, code, passed)
                    here = (sender == me) & (j < amount)
                    at = SEND + new_times[j]
                    plan[at] = plan[at] ^ jnp.where(here, (code ^ 255) << shift, 0)
                    here = (receiver == me) & (j < amount)
                    place = jnp.where(
                        dst == me, OWNED + (slot & 1) * 8 + begin + j, slot_now + j
                    )
                    at = KEEP + new_times[j] + LAG
                    plan[at] = plan[at] ^ jnp.where(here, (place ^ 255) << shift, 0)
                    at = jnp.where(here & (dst == me), LAST + place - OWNED, PLAN - 1)
                    plan[at] = new_times[j] + LAG
                kept = (receiver == me) & (dst != me)
                var[zs + 2] = slot_now + jnp.where(kept, amount, 0)

            return (*new_times, kind, slot_now)

        early = jnp.int32(-LAG)
        state = lax.fori_loop(0, hops, hop, (early, early, early, early, jnp.int32(0), jnp.int32(0)))
        end = jnp.maximum(jnp.maximum(state[0], state[1]), jnp.maximum(state[2], state[3]))
        for j in range(4):
            end = jnp.where(j == amount - 1, state[j], end)
        var[zs + 3] = jnp.maximum(var[zs + 3], end + 1)

    def by_hops(k, _):
        hops = zs + 1 - k

        def each(index, _):
            stream(hops, index)
            return 0

        lax.fori_loop(0, var[hops], each, 0)
        return 0

    lax.fori_loop(0, zs + 1, by_hops, 0)

    plan[META + 2 * N_META] = var[zs + 3]
    blank(False)


def make_plan(zs, where, lengths, slot_of, query, fresh, kv):
    steps, items, heads, width = query.shape
    rows = 2 * steps * heads
    return pl.pallas_call(
        functools.partial(plan_kernel, zs),
        in_specs=[SMEM] * 3 + [VMEM] * 2,
        out_specs=[SMEM] + [ANY] * 3 + [VMEM] * 2,
        out_shape=[
            jax.ShapeDtypeStruct((PLAN,), jnp.int32),
            pltpu.HBM((SLOTS + 16, width, CHUNK), kv.dtype),
            pltpu.HBM(kv.shape, kv.dtype),
            pltpu.HBM((items, width, 4 * CHUNK), kv.dtype),
            pltpu.VMEM((items, rows, DL), jnp.float32),
            pltpu.VMEM((items, 2, rows, 128), jnp.float32),
        ],
        scratch_shapes=[
            pltpu.SMEM((6 * zs * (TMAX // 32 + 1),), jnp.int32),
            pltpu.SMEM((6 * zs,), jnp.int32),
            pltpu.SMEM(((zs + 2) * 8 * zs,), jnp.int32),
            pltpu.SMEM((9 * 4 * zs,), jnp.int32),
            pltpu.SMEM((zs + 4 + 9,), jnp.int32),
            pltpu.VMEM((width, CHUNK), kv.dtype),
            pltpu.SemaphoreType.DMA((16,)),
        ],
        compiler_params=SMALL,
    )(where, lengths, slot_of, query, fresh)


def lanes(index):
    return pl.ds(pl.multiple_of(index * CHUNK, CHUNK), CHUNK)


def hand_kernel(where, lengths, kv, out, sems):
    for start in (True, False):
        for item in range(2):
            n = cdiv(lengths[where[0] * 2 + item], CHUNK)
            first = jnp.minimum(cdiv(n, 2), 4)
            for q in range(4):
                copy = pltpu.make_async_copy(
                    kv.at[item, :, lanes(first + q)],
                    out.at[item, :, pl.ds(q * CHUNK, CHUNK)],
                    sems.at[item * 4 + q],
                )
                if start:
                    copy.start()
                else:
                    copy.wait()


def hand_over(where, lengths, kv):
    return pl.pallas_call(
        hand_kernel,
        in_specs=[SMEM, SMEM, ANY],
        out_specs=VMEM,
        out_shape=pltpu.VMEM((2, kv.shape[1], 4 * CHUNK), kv.dtype),
        scratch_shapes=[pltpu.SemaphoreType.DMA((8,))],
        compiler_params=SMALL,
    )(where, lengths, kv)


def owned_chunk(plan, code):
    item, j = (code >> 3) & 1, code & 7
    at = META + item * N_META
    ident = plan[at + 2] + j
    return item, j, ident, ident < plan[at + 1]


def store_owned(plan, head, code, rows, cache, post, sem, start):
    item, j, ident, real = owned_chunk(plan, code)
    per_half = 2048 // CHUNK
    here = ident >> 3 == head

    @pl.when(real & here)
    def _():
        copy = pltpu.make_async_copy(rows, cache.at[item, :, lanes(ident & (per_half - 1))], sem)
        copy.start() if start else copy.wait()

    @pl.when(real & ~here)
    def _():
        copy = pltpu.make_async_copy(rows, post.at[item, :, lanes(j & 3)], sem)
        copy.start() if start else copy.wait()


def step_kernel(taking, time, where, plan, kv, pre, *refs):
    if taking:
        query, query_other, *refs = refs
        arrived, refs = refs[:3], refs[8:]
        sends, inbox, (cache, post, total, stats, local, sems) = refs[:3], refs[3], refs[4:]
    else:
        arrived, refs = refs[:3], refs[4:]
        sends, (inbox, sems) = refs[:3], refs[3:]
    head = where[1]
    to_send, to_keep = plan[SEND + time[0]], plan[KEEP + time[0]]
    codes = [(to_send >> (8 * kind)) & 255 for kind in range(3)]
    places = [(to_keep >> (8 * kind)) & 255 for kind in range(3)]
    waiting = OWNED if taking else NOTHING

    def load_from(source, kind):
        return pltpu.make_async_copy(source, sends[kind], sems.at[kind])

    def keep(kind):
        place = jnp.minimum(places[kind], SLOTS + 15)
        return pltpu.make_async_copy(arrived[kind], inbox.at[place], sems.at[3 + kind])

    for kind in range(3):
        code = codes[kind]

        @pl.when(code < FROM_PRE)
        def _():
            load_from(kv.at[code >> 3, :, lanes(code & 7)], kind).start()

        @pl.when((code >= FROM_PRE) & (code < FROM_LINK))
        def _():
            load_from(pre.at[(code - FROM_PRE) >> 2, :, lanes(code & 3)], kind).start()

        for other in range(3):

            @pl.when(code == FROM_LINK + other)
            def _():
                load_from(arrived[other], kind).start()

        @pl.when((code >= FROM_INBOX) & (code < NOTHING))
        def _():
            load_from(inbox.at[code - FROM_INBOX], kind).start()

        @pl.when(places[kind] < waiting)
        def _():
            keep(kind).start()

    if taking:
        staying = plan[STAY + time[0]]

        def load_local():
            item = (staying >> 3) & 1
            source = jnp.maximum(plan[META + item * N_META + 4], 0)
            return pltpu.make_async_copy(kv.at[source, :, lanes(staying & 7)], local, sems.at[6])

        @pl.when(staying >= 0)
        def _():
            load_local().start()

        def take(code, rows, sem):
            store_owned(plan, head, code, rows, cache, post, sem, True)
            item, j, _, _ = owned_chunk(plan, code)
            absorb(plan, item, j, rows, query, query_other, total, stats)

        for kind in range(3):

            @pl.when((places[kind] >= OWNED) & (places[kind] < NOTHING))
            def _():
                take(places[kind] - OWNED, arrived[kind], sems.at[3 + kind])

        @pl.when(staying >= 0)
        def _():
            load_local().wait()
            take(staying, local, sems.at[7])
            store_owned(plan, head, staying, local, cache, post, sems.at[7], False)

    for kind in range(3):

        @pl.when(codes[kind] < NOTHING)
        def _():
            load_from(arrived[kind], kind).wait()

        @pl.when(places[kind] < waiting)
        def _():
            keep(kind).wait()

        if taking:

            @pl.when((places[kind] >= OWNED) & (places[kind] < NOTHING))
            def _():
                code = places[kind] - OWNED
                store_owned(plan, head, code, arrived[kind], cache, post, sems.at[3 + kind], False)


def in_hbm(arrays):
    return [pltpu.with_memory_space_constraint(a, pltpu.HBM) for a in arrays]


def in_vmem(arrays):
    return [pltpu.with_memory_space_constraint(a, pltpu.VMEM) for a in arrays]


def like(state):
    shapes = [pltpu.HBM(a.shape, a.dtype) for a in state[:3]]
    return shapes + [pltpu.VMEM(a.shape, a.dtype) for a in state[3:]]


def one_step(taking, time, where, plan, kv, pre, queries, arrived, state):
    inbox = state[0]
    piece = pltpu.VMEM(inbox.shape[1:], inbox.dtype)
    queries = queries if taking else ()
    state = state if taking else state[:1]
    first = 5 + len(queries) + 3
    wide = [ANY] * 3 + [VMEM] * 2 if taking else [ANY]
    scratch = [pltpu.VMEM(inbox.shape[1:], inbox.dtype)] if taking else []
    out = pl.pallas_call(
        functools.partial(step_kernel, taking),
        in_specs=[SMEM] * 3 + [ANY] * 2 + [VMEM] * (len(queries) + 3) + wide,
        out_specs=[VMEM] * 3 + wide,
        out_shape=[piece] * 3 + like(state),
        input_output_aliases={first + k: 3 + k for k in range(len(state))},
        scratch_shapes=scratch + [pltpu.SemaphoreType.DMA((8,))],
        compiler_params=SMALL,
        cost_estimate=pl.CostEstimate(
            flops=0, bytes_accessed=12 * inbox.shape[1] * CHUNK, transcendentals=0
        ),
    )(
        time, where, plan, *in_hbm([kv, pre]), *in_vmem([*queries, *arrived]),
        *in_hbm(state[:3]), *in_vmem(state[3:]),
    )
    return out[:3], out[3:]


def finish_kernel(time, where, plan, query, query_other, inbox, *refs):
    arrived, refs = refs[: 3 * LAG], refs[3 * LAG + 4 :]
    cache, post, total, stats, other_sum, other_stats, local, sems = refs
    head = where[1]
    own = other_sum.shape[1]

    def take_waiting(code, _):
        row = plan[LAST + code]

        @pl.when((row >= UNROLLED) & (row < time[0]))
        def _():
            load = pltpu.make_async_copy(inbox.at[OWNED + code], local, sems.at[3 * LAG])
            load.start()
            load.wait()
            store_owned(plan, head, code, local, cache, post, sems.at[3 * LAG], True)
            item, j, _, _ = owned_chunk(plan, code)
            absorb(plan, item, j, local, query, query_other, total, stats)
            store_owned(plan, head, code, local, cache, post, sems.at[3 * LAG], False)

        return 0

    @pl.when(time[0] > UNROLLED)
    def _():
        lax.fori_loop(0, 16, take_waiting, 0)

    for start in (True, False):
        for late in range(LAG):
            word = plan[KEEP + time[0] + late]
            for kind in range(3):
                place = (word >> (8 * kind)) & 255
                rows = arrived[3 * late + kind]
                code = place - OWNED

                @pl.when((place >= OWNED) & (place < NOTHING))
                def _():
                    sem = sems.at[3 * late + kind]
                    store_owned(plan, head, code, rows, cache, post, sem, start)
                    if start:
                        item, j, _, _ = owned_chunk(plan, code)
                        absorb(plan, item, j, rows, query, query_other, total, stats)

    for item in range(other_sum.shape[0]):
        others = pl.ds(own, own)
        other_sum[item] = total[item, others, :].astype(other_sum.dtype)
        lane = lax.broadcasted_iota(jnp.int32, (own, 128), 1)
        other_stats[item] = jnp.where(
            lane == 0, stats[item, 0, others, :], stats[item, 1, others, :]
        )


def finish(time, where, plan, query, query_other, arrived, state):
    items, rows, width = state[3].shape
    shapes = like(state)[1:]
    return pl.pallas_call(
        finish_kernel,
        in_specs=[SMEM] * 3 + [VMEM] * 2 + [ANY] + [VMEM] * (3 * LAG) + [ANY] * 2 + [VMEM] * 2,
        out_specs=[ANY] * 2 + [VMEM] * 4,
        out_shape=shapes
        + [
            pltpu.VMEM((items, rows // 2, width), jnp.bfloat16),
            pltpu.VMEM((items, rows // 2, 128), jnp.float32),
        ],
        input_output_aliases={6 + 3 * LAG + k: k for k in range(4)},
        scratch_shapes=[
            pltpu.VMEM(state[0].shape[1:], state[0].dtype),
            pltpu.SemaphoreType.DMA((3 * LAG + 1,)),
        ],
        compiler_params=SMALL,
    )(
        time, where, plan, *in_vmem([query, query_other]), *in_hbm(state[:1]), *in_vmem(arrived),
        *in_hbm(state[1:3]), *in_vmem(state[3:]),
    )


def return_kernel(where, plan, post, _, cache, sems):
    per_half = 2048 // CHUNK
    for start in (True, False):
        for item in range(2):
            at = META + item * N_META
            n, stays, h = plan[at + 1], plan[at + 4], plan[at + 5]
            for q in range(4):

                @pl.when((where[1] == 0) & (stays < 0) & (h + q < jnp.minimum(n, per_half)))
                def _():
                    copy = pltpu.make_async_copy(
                        post.at[item, :, pl.ds(q * CHUNK, CHUNK)],
                        cache.at[item, :, lanes(jnp.minimum(h + q, per_half - 1))],
                        sems.at[item * 4 + q],
                    )
                    copy.start() if start else copy.wait()


def return_rows(where, plan, post, cache):
    return pl.pallas_call(
        return_kernel,
        in_specs=[SMEM, SMEM, VMEM, ANY],
        out_specs=ANY,
        out_shape=jax.ShapeDtypeStruct(cache.shape, cache.dtype),
        input_output_aliases={3: 0},
        scratch_shapes=[pltpu.SemaphoreType.DMA((8,))],
    )(where, plan, post, *in_hbm([cache]))


def merge_kernel(total, stats, other_sum, other_stats, out):
    items, own, _ = other_sum.shape
    steps, _, heads, _ = out.shape
    mine = pl.ds(0, own)
    for item in range(items):
        top_one, sum_one = stats[item, 0, mine, :][:, :1], stats[item, 1, mine, :][:, :1]
        top_two, sum_two = other_stats[item][:, :1], other_stats[item][:, 1:2]
        top = jnp.maximum(top_one, top_two)
        scale_one = jnp.exp(top_one - top)
        scale_two = jnp.exp(top_two - top)
        weight_sum = sum_one * scale_one + sum_two * scale_two
        summed = total[item, mine, :] * scale_one
        summed = summed + other_sum[item].astype(jnp.float32) * scale_two
        result = (summed / weight_sum).astype(out.dtype)
        for step in range(steps):
            out[step, item] = result[step * heads : (step + 1) * heads]


def merge(total, stats, other_sum, other_stats, steps, heads):
    return pl.pallas_call(
        merge_kernel,
        in_specs=[VMEM] * 4,
        out_specs=VMEM,
        out_shape=jax.ShapeDtypeStruct((steps, total.shape[0], heads, DL), jnp.bfloat16),
        compiler_params=SMALL,
    )(*in_vmem([total, stats, other_sum, other_stats]))


def exchanges(zs):
    even, odd, across = [], [], []
    for z in range(zs):
        for y in range(2):
            across.append((z * 2 + y, z * 2 + 1 - y))
            if z + 1 < zs:
                pairs = even if z % 2 == 0 else odd
                pairs.append((z * 2 + y, z * 2 + 2 + y))
                pairs.append((z * 2 + 2 + y, z * 2 + y))
    return even, odd, across


def routed(zs, kv, lengths, slot_of, query, new_latent):
    kinds = exchanges(zs)
    steps, items, heads, width = query.shape
    where = jnp.stack([lax.axis_index("seq"), lax.axis_index("head")]).astype(jnp.int32)
    kv = jnp.swapaxes(kv, 1, 2)
    swap = [(0, 1), (1, 0)]
    pre = lax.ppermute(hand_over(where, lengths, kv), "head", [(0, 1)])
    query_other = lax.ppermute(query, "head", swap)
    fresh = jnp.pad(jnp.swapaxes(new_latent, 0, 1), ((0, 0), (0, 128 - steps), (0, 0)))
    plan, *state = make_plan(zs, where, lengths, slot_of, query, fresh, kv)
    plan, query_other = lax.optimization_barrier((plan, query_other))

    def run(taking, begin, count, arrived, state):
        for k in range(count):
            time = jnp.full((1,), begin + k, jnp.int32)
            queries = (query, query_other)
            sends, state = one_step(
                taking, time, where, plan, kv, pre, queries, arrived[0], state
            )
            new = [lax.ppermute(s, "seq", pairs) for s, pairs in zip(sends, kinds)]
            arrived = arrived[1:] + [new]
        return arrived, state

    nothing = [jnp.zeros((width, CHUNK), kv.dtype)] * 3
    arrived, state = run(True, 0, UNROLLED, [nothing] * LAG, state)
    last_step = plan[META + 2 * N_META]

    def more(carry):
        return carry[0] < last_step

    def body(carry):
        time, arrived, inbox = carry
        arrived, (inbox,) = run(False, time, BODY, arrived, [inbox])
        return time + BODY, arrived, inbox

    inbox, *state = state
    time, arrived, inbox = lax.while_loop(more, body, (jnp.int32(UNROLLED), arrived, inbox))
    cache, post, total, stats, other_sum, other_stats = finish(
        time[None], where, plan, query, query_other, sum(arrived, []), [inbox, *state]
    )
    post = lax.ppermute(post, "head", [(1, 0)])
    other_sum = lax.ppermute(other_sum, "head", swap)
    other_stats = lax.ppermute(other_stats, "head", swap)
    attended = merge(total, stats, other_sum, other_stats, steps, heads)
    cache = return_rows(where, plan, post, cache)
    return attended, jnp.swapaxes(cache, 1, 2)


def merged_2(shard, axis, combine):
    everything = jax.tree.map(
        lambda part, kind: lax.all_gather(part.astype(kind), axis),
        shard,
        (jnp.bfloat16, jnp.bfloat16, jnp.bfloat16),
    )

    def take(k):
        return jax.tree.map(lambda part, own: part[k].astype(own.dtype), everything, shard)

    return lax.fori_loop(
        1, lax.axis_size(axis), lambda k, so_far: combine(so_far, take(k)), take(0)
    )


def join_partials(first, second):
    top = jnp.maximum(first[0], second[0])
    scale_one = jnp.exp(first[0] - top)
    scale_two = jnp.exp(second[0] - top)
    total = first[1] * scale_one + second[1] * scale_two
    summed = first[2] * scale_one[..., None] + second[2] * scale_two[..., None]
    return (top, total, summed)


def balanced(kv, lengths, slot_of, query, new_latent):
    req = kv.shape[0]
    half = kv.shape[1]
    count = lengths.shape[0]
    steps_new = query.shape[0]
    heads_here = query.shape[2]
    pieces = lax.all_to_all(kv, "seq", split_axis=1, concat_axis=0, tiled=True)
    inverse = jnp.zeros((count,), jnp.int32).at[slot_of].set(jnp.arange(count, dtype=jnp.int32))
    ordered = jnp.take(pieces, inverse, axis=0)
    cache = lax.all_to_all(ordered, "seq", split_axis=0, concat_axis=1, tiled=True)
    my_lens = lax.dynamic_slice_in_dim(
        jnp.take(lengths, inverse, axis=0), lax.axis_index("seq") * req, req
    )
    head_pos = lax.axis_index("head")
    rows = steps_new * heads_here
    row_step = jnp.arange(rows, dtype=jnp.int32) // heads_here
    valid_two = jnp.arange(steps_new, dtype=jnp.int32)[None, :] <= row_step[:, None]
    results = []
    every_query = lax.all_gather(query, "head", axis=2, tiled=True)
    heads_all = every_query.shape[2]
    rows_all = steps_new * heads_all
    positions = head_pos * half + jnp.arange(half, dtype=jnp.int32)
    tops = []
    totals = []
    sums = []
    for item in range(req):
        queries = every_query[:, item].reshape(rows_all, every_query.shape[3])
        valid_one = positions[None, :] < my_lens[item]
        cache_scores = (
            jnp.einsum("nd,td->nt", queries, cache[item], preferred_element_type=jnp.float32)
            * score_scale
        )
        top = jnp.max(jnp.where(valid_one, cache_scores, big_negative), axis=1)
        weight_one = jnp.where(valid_one, jnp.exp(cache_scores - top[:, None]), 0.0)
        tops.append(top)
        totals.append(jnp.sum(weight_one, axis=1))
        sums.append(
            jnp.dot(
                weight_one.astype(jnp.bfloat16),
                cache[item][:, :DL],
                preferred_element_type=jnp.float32,
            )
        )
    merged = merged_2((jnp.stack(tops), jnp.stack(totals), jnp.stack(sums)), "head", join_partials)
    start = head_pos * heads_here
    own_top = lax.dynamic_slice_in_dim(
        merged[0].reshape(req, steps_new, heads_all), start, heads_here, 2
    ).reshape(req, rows)
    own_total = lax.dynamic_slice_in_dim(
        merged[1].reshape(req, steps_new, heads_all), start, heads_here, 2
    ).reshape(req, rows)
    own_sum = lax.dynamic_slice_in_dim(
        merged[2].reshape(req, steps_new, heads_all, DL), start, heads_here, 2
    ).reshape(req, rows, DL)
    for item in range(req):
        queries = query[:, item].reshape(rows, query.shape[3])
        fresh = new_latent[:, item]
        new_scores = (
            jnp.einsum("nd,td->nt", queries, fresh, preferred_element_type=jnp.float32)
            * score_scale
        )
        top = jnp.maximum(
            own_top[item], jnp.max(jnp.where(valid_two, new_scores, big_negative), axis=1)
        )
        rescale = jnp.exp(own_top[item] - top)
        weight_two = jnp.where(valid_two, jnp.exp(new_scores - top[:, None]), 0.0)
        total = own_total[item] * rescale + jnp.sum(weight_two, axis=1)
        summed = own_sum[item] * rescale[:, None]
        summed = summed + jnp.dot(
            weight_two.astype(jnp.bfloat16), fresh[:, :DL], preferred_element_type=jnp.float32
        )
        results.append(
            (summed / total[:, None]).astype(jnp.bfloat16).reshape(steps_new, heads_here, DL)
        )
    return (jnp.stack(results, axis=1), cache)


def solution(mesh):
    local = functools.partial(routed, 4) if mesh.shape["seq"] == 8 else balanced
    return jax.shard_map(
        local,
        mesh=mesh,
        in_specs=(
            P(("groups", "seq"), "head", None),
            P("groups"),
            P("groups"),
            P(None, ("groups", "seq"), "head", None),
            P(None, ("groups", "seq"), None),
        ),
        out_specs=(P(None, ("groups", "seq"), "head", None), P(("groups", "seq"), "head", None)),
        check_vma=False,
    )
```

```python
import functools

import jax
import jax.numpy as jnp
from jax import lax
from jax.experimental import pallas as pl
from jax.experimental.pallas import tpu as pltpu
from jax.sharding import PartitionSpec as P

DL = 512
CHUNK_BITS = 8
CHUNK = 1 << CHUNK_BITS
LAG = 2
TMAX = 256
UNROLLED = 16
BODY = 3
SLOTS = 160

score_scale = 192.0 ** (-0.5)
big_negative = -1e30

ANY = pl.BlockSpec(memory_space=pl.ANY)
VMEM = pl.BlockSpec(memory_space=pltpu.VMEM)
SMEM = pl.BlockSpec(memory_space=pltpu.SMEM)

SMALL = pltpu.CompilerParams(vmem_limit_bytes=8 * 2**20)

FROM_KV, FROM_PRE, FROM_LINK, FROM_INBOX, NOTHING = 0, 16, 24, 32, 255
OWNED = SLOTS

SEND, KEEP, STAY, LAST, META = 0, TMAX, 2 * TMAX, 2 * TMAX + 16, 2 * TMAX + 32
N_META = 8
HEAD = META + 2 * N_META + 1
PLAN = META + 2 * N_META + 8


def cdiv(a, b):
    return (a + b - 1) // b


def nt_dot(a, b):
    return lax.dot_general(a, b, (((1,), (1,)), ((), ())), preferred_element_type=jnp.float32)


def head_rows(query, item):
    return jnp.concatenate([query[step, item] for step in range(query.shape[0])], axis=0)


def begin_sums(query, fresh, total, stats):
    steps, items, heads, _ = query.shape
    own = steps * heads
    for item in range(items):
        new = fresh[item]
        step_of = lax.broadcasted_iota(jnp.int32, (own, new.shape[0]), 0) // heads
        position = lax.broadcasted_iota(jnp.int32, (own, new.shape[0]), 1)
        valid = position <= step_of
        scores = nt_dot(head_rows(query, item), new) * score_scale
        scores = jnp.where(valid, scores, big_negative)
        top = jnp.max(scores, axis=1, keepdims=True)
        weight = jnp.where(valid, jnp.exp(scores - top), 0.0)
        mine, others = pl.ds(0, own), pl.ds(own, own)
        stats[item, 0, mine, :] = jnp.broadcast_to(top, (own, 128))
        stats[item, 1, mine, :] = jnp.broadcast_to(
            jnp.sum(weight, axis=1, keepdims=True), (own, 128)
        )
        total[item, mine, :] = jnp.dot(
            weight.astype(jnp.bfloat16), new[:, :DL], preferred_element_type=jnp.float32
        )
        stats[item, 0, others, :] = jnp.full((own, 128), big_negative, jnp.float32)
        stats[item, 1, others, :] = jnp.zeros((own, 128), jnp.float32)
        total[item, others, :] = jnp.zeros((own, DL), jnp.float32)


def absorb(plan, item, j, keys, query, query_other, total, stats):
    at = META + item * N_META
    left = plan[at] - (plan[at + 2] + j) * CHUNK

    @pl.when(left > 0)
    def _():
        queries = jnp.concatenate([head_rows(query, item), head_rows(query_other, item)], axis=0)
        scores = jnp.dot(queries, keys[...], preferred_element_type=jnp.float32) * score_scale
        inside = lax.broadcasted_iota(jnp.int32, scores.shape, 1) < left
        scores = jnp.where(inside, scores, big_negative)
        before = stats[item, 0]
        top = jnp.maximum(before, jnp.max(scores, axis=1, keepdims=True))
        scale = jnp.exp(before - top)
        weight = jnp.exp(scores - jnp.concatenate([top] * (CHUNK // 128), axis=1))
        stats[item, 0] = top
        stats[item, 1] = stats[item, 1] * scale + jnp.sum(weight, axis=1, keepdims=True)
        added = nt_dot(weight.astype(jnp.bfloat16), keys[pl.ds(0, DL), :])
        total[item] = total[item] * jnp.concatenate([scale] * (DL // 128), axis=1) + added


def plan_kernel(
    zs, where, lengths, slot_of, query, fresh,
    plan, inbox, cache, post, total, stats,
    busy, load, bucket, by_size, var, zeros, sems,
):
    me, head = where[0], where[1]
    words = TMAX // 32 + 1
    count = 4 * zs
    per_half = 2048 // CHUNK
    streams = 2 * count

    def fill(ref, begin, size, value):
        wide = 8
        assert size % wide == 0

        def some(i, _):
            for k in range(wide):
                ref[begin + i * wide + k] = value
            return 0

        lax.fori_loop(0, size // wide, some, 0)

    def sizes(r):
        n = (lengths[r] + CHUNK - 1) >> CHUNK_BITS
        return n, (n + 1) >> 1

    fill(plan, 0, 2 * TMAX + 32, jnp.int32(-1))

    var[0] = 0

    def slots(r, _):
        @pl.when(slot_of[r] >> 1 == me)
        def _():
            item = slot_of[r] & 1
            at = META + item * N_META
            n, h = sizes(r)
            stays = r >> 1 == me
            base = jnp.where(head == 0, 0, jnp.where(stays, per_half, h))
            end = jnp.where(
                stays,
                jnp.where(head == 0, jnp.minimum(n, per_half), n),
                jnp.where(head == 0, h, n),
            )
            held = jnp.maximum(end - base, 0)
            plan[at] = lengths[r]
            plan[at + 1] = n
            plan[at + 2] = base
            plan[at + 3] = held
            plan[at + 4] = jnp.where(stays, r & 1, -1)
            plan[at + 5] = h

            def staying(j, _):
                plan[STAY + var[0] + j] = item * 8 + j
                return 0

            staying_here = jnp.where(stays, held, 0)
            lax.fori_loop(0, staying_here, staying, 0)
            var[0] = var[0] + staying_here

        return 0

    lax.fori_loop(0, count, slots, 0)

    zeros[...] = jnp.zeros_like(zeros)

    def blank(start):
        for item in range(2):
            n = plan[META + item * N_META + 1]
            for c in range(per_half):

                @pl.when(head * per_half + c >= n)
                def _():
                    copy = pltpu.make_async_copy(
                        zeros,
                        cache.at[item, :, pl.ds(c * CHUNK, CHUNK)],
                        sems.at[item * per_half + c],
                    )
                    copy.start() if start else copy.wait()

    blank(True)
    begin_sums(query, fresh, total, stats)
    fill(busy, 0, 6 * zs * words, jnp.int32(0))
    for i in range(6 * zs):
        load[i] = 0
    for i in range(zs + 2):
        var[i] = 0
    var[zs + 2] = 0
    var[zs + 3] = 0

    def y_link(z, y):
        return 4 * zs + z * 2 + y

    for i in range(9):
        var[zs + 4 + i] = 0

    def sort(r, _):
        h = sizes(r)[1]
        filled = var[zs + 4 + h]
        by_size[h * count + filled] = r
        var[zs + 4 + h] = filled + 1
        return 0

    lax.fori_loop(0, count, sort, 0)

    def route(r):
        src = r >> 1
        dst = slot_of[r] >> 1
        n, h = sizes(r)
        z0, y0 = src >> 1, src & 1
        z1, y1 = dst >> 1, dst & 1
        low, high = jnp.minimum(z0, z1), jnp.maximum(z0, z1)
        offset = jnp.where(z1 > z0, 0, 2 * zs)
        inside = [(low <= z) & (z < high) for z in range(zs - 1)]
        turn = jnp.where(y0 == y1, 0, 1)
        for part in range(2):
            amount = jnp.where(src == dst, 0, h >> 1 if part == 0 else h - (h >> 1))

            def cost(col):
                top = jnp.int32(0)
                for z in range(zs - 1):
                    top = jnp.maximum(top, jnp.where(inside[z], load[offset + z * 2 + col], 0))
                return top

            straight = jnp.maximum(cost(y0), jnp.where(turn == 1, load[y_link(z1, y0)], 0))
            other = jnp.maximum(cost(1 - y0), load[y_link(z0, y0)])
            other = jnp.where(
                turn == 1, other, jnp.maximum(other, load[y_link(z1, 1 - y0)])
            )
            col = jnp.where((z0 != z1) & (other < straight), 1 - y0, y0)
            for z in range(zs - 1):
                at = offset + z * 2 + col
                load[at] = load[at] + jnp.where(inside[z], amount, 0)
            first = jnp.where(col != y0, 1, 0)
            last = jnp.where(col != y1, 1, 0)
            at = y_link(z0, y0)
            load[at] = load[at] + first * amount
            at = y_link(z1, col)
            load[at] = load[at] + last * amount
            hops = jnp.where(amount == 0, 0, high - low + first + last)
            filled = var[hops]
            bucket[hops * streams + filled] = r * 4 + part * 2 + col
            var[hops] = filled + 1

    def routes(k, _):
        h = per_half - k

        def each(index, _):
            route(by_size[h * count + index])
            return 0

        lax.fori_loop(0, var[zs + 4 + h], each, 0)
        return 0

    lax.fori_loop(0, per_half, routes, 0)

    def stream(hops, index):
        packed = bucket[hops * streams + index]
        r, part, col = packed >> 2, (packed >> 1) & 1, packed & 1
        src = r >> 1
        slot = slot_of[r]
        dst = slot >> 1
        n, h = sizes(r)
        half = h >> 1
        begin = jnp.where(part == 0, 0, half)
        amount = jnp.where(part == 0, half, h - half)
        item = r & 1
        z0, y0 = src >> 1, src & 1
        z1 = dst >> 1
        up = jnp.where(z1 > z0, 1, 0)
        sign = 2 * up - 1
        first = jnp.where(col != y0, 1, 0)
        dz = jnp.abs(z1 - z0)

        def hop(i, state):
            times, kind_before, slot_before = state[:4], state[4], state[5]
            is_first = i < first
            is_last = i >= first + dz
            z = z0 + sign * (i - first)
            edge = z + up - 1
            is_y = is_first | is_last
            z_turn = jnp.where(is_first, z0, z1)
            y_from = jnp.where(is_first, y0, col)
            link = jnp.where(
                is_y, y_link(z_turn, y_from), jnp.where(up == 1, 0, 2 * zs) + edge * 2 + col
            )
            kind = jnp.where(is_y, 2, edge & 1)
            sender = jnp.where(is_y, z_turn, z) * 2 + y_from
            sender = jnp.where(is_y, sender, z * 2 + col)
            receiver = jnp.where(is_y, z_turn * 2 + 1 - y_from, (z + sign) * 2 + col)
            row = link * words

            start = times[0] + LAG
            word, shift = start >> 5, start & 31
            low_word, high_word = busy[row + word], busy[row + word + 1]
            free = ~(lax.shift_right_logical(low_word, shift) | ((high_word << 1) << (31 - shift)))
            used, fits, quick = jnp.int32(0), jnp.bool_(True), []
            for j in range(4):
                placed = j < amount
                wait = times[j] - times[0]
                allowed = free & (jnp.int32(-1) << jnp.minimum(wait, 31))
                lowest = allowed & -allowed
                fits = fits & ((placed & (allowed != 0) & (wait < 32)) | ~placed)
                lowest = jnp.where(placed, lowest, 0)
                free = free & ~lowest
                used = used | lowest
                time = start + 31 - lax.clz(lowest)
                quick.append(time if j == 0 else jnp.where(placed, time, quick[-1]))

            def in_window():
                busy[row + word] = low_word | (used << shift)
                busy[row + word + 1] = high_word | lax.shift_right_logical(
                    lax.shift_right_logical(used, 1), 31 - shift
                )
                return tuple(quick)

            def beyond():
                found = []
                for j in range(4):
                    begin_at = times[j] + LAG
                    word0 = begin_at >> 5
                    free0 = ~busy[row + word0] & (jnp.int32(-1) << (begin_at & 31))

                    def onward(state):
                        word = state[0] + 1
                        return word, ~busy[row + word]

                    at, free = lax.while_loop(lambda s: s[1] == 0, onward, (word0, free0))
                    lowest = free & -free
                    busy[row + at] = busy[row + at] | jnp.where(j < amount, lowest, 0)
                    time = at * 32 + 31 - lax.clz(lowest)
                    found.append(time if j == 0 else jnp.where(j < amount, time, found[-1]))
                return tuple(found)

            new_times = lax.cond(fits, in_window, beyond)
            slot_now = var[zs + 2]

            @pl.when((sender == me) | (receiver == me))
            def _():
                shift = kind * 8
                for j in range(4):
                    ident = begin + j + jnp.where(head == 0, 0, h)
                    own = FROM_KV + item * per_half + (ident & (per_half - 1))
                    handed = FROM_PRE + item * 4 + ident - jnp.minimum(h, 4)
                    code = jnp.where((head == 1) & (ident < per_half), handed, own)
                    passed = jnp.where(
                        new_times[j] == times[j] + LAG,
                        FROM_LINK + kind_before,
                        FROM_INBOX + slot_before + j,
                    )
                    code = jnp.where(i == 0, code, passed)
                    here = (sender == me) & (j < amount)
                    at = SEND + new_times[j]
                    plan[at] = plan[at] ^ jnp.where(here, (code ^ 255) << shift, 0)
                    here = (receiver == me) & (j < amount)
                    place = jnp.where(
                        dst == me, OWNED + (slot & 1) * 8 + begin + j, slot_now + j
                    )
                    at = KEEP + new_times[j] + LAG
                    plan[at] = plan[at] ^ jnp.where(here, (place ^ 255) << shift, 0)
                    at = jnp.where(here & (dst == me), LAST + place - OWNED, PLAN - 1)
                    plan[at] = new_times[j] + LAG
                kept = (receiver == me) & (dst != me)
                var[zs + 2] = slot_now + jnp.where(kept, amount, 0)

            return (*new_times, kind, slot_now)

        early = jnp.int32(-LAG)
        state = lax.fori_loop(0, hops, hop, (early, early, early, early, jnp.int32(0), jnp.int32(0)))
        end = jnp.maximum(jnp.maximum(state[0], state[1]), jnp.maximum(state[2], state[3]))
        for j in range(4):
            end = jnp.where(j == amount - 1, state[j], end)
        var[zs + 3] = jnp.maximum(var[zs + 3], end + 1)

    def by_hops(k, _):
        hops = zs + 1 - k

        def each(index, _):
            stream(hops, index)
            return 0

        lax.fori_loop(0, var[hops], each, 0)
        return 0

    lax.fori_loop(0, zs + 1, by_hops, 0)

    plan[META + 2 * N_META] = var[zs + 3]
    plan[HEAD] = head
    blank(False)


def make_plan(zs, where, lengths, slot_of, query, fresh, kv):
    steps, items, heads, width = query.shape
    rows = 2 * steps * heads
    return pl.pallas_call(
        functools.partial(plan_kernel, zs),
        in_specs=[SMEM] * 3 + [VMEM] * 2,
        out_specs=[SMEM] + [ANY] * 3 + [VMEM] * 2,
        out_shape=[
            pltpu.SMEM((PLAN,), jnp.int32),
            pltpu.HBM((SLOTS + 16, width, CHUNK), kv.dtype),
            pltpu.HBM(kv.shape, kv.dtype),
            pltpu.HBM((items, width, 4 * CHUNK), kv.dtype),
            pltpu.VMEM((items, rows, DL), jnp.float32),
            pltpu.VMEM((items, 2, rows, 128), jnp.float32),
        ],
        scratch_shapes=[
            pltpu.SMEM((6 * zs * (TMAX // 32 + 1),), jnp.int32),
            pltpu.SMEM((6 * zs,), jnp.int32),
            pltpu.SMEM(((zs + 2) * 8 * zs,), jnp.int32),
            pltpu.SMEM((9 * 4 * zs,), jnp.int32),
            pltpu.SMEM((zs + 4 + 9,), jnp.int32),
            pltpu.VMEM((width, CHUNK), kv.dtype),
            pltpu.SemaphoreType.DMA((16,)),
        ],
        compiler_params=SMALL,
    )(where, lengths, slot_of, query, fresh)


def lanes(index):
    return pl.ds(pl.multiple_of(index * CHUNK, CHUNK), CHUNK)


def hand_kernel(where, lengths, kv, out, sems):
    def hand(start):
        for item in range(2):
            n = (lengths[where[0] * 2 + item] + CHUNK - 1) >> CHUNK_BITS
            h = (n + 1) >> 1
            for q in range(4):
                ident = jnp.minimum(h, 4) + q

                @pl.when((ident >= h) & (ident < n))
                def _():
                    copy = pltpu.make_async_copy(
                        kv.at[item, :, lanes(ident)],
                        out.at[item, :, pl.ds(q * CHUNK, CHUNK)],
                        sems.at[item * 4 + q],
                    )
                    copy.start() if start else copy.wait()

    hand(True)
    hand(False)


def hand_over(where, lengths, kv):
    return pl.pallas_call(
        hand_kernel,
        in_specs=[SMEM, SMEM, ANY],
        out_specs=VMEM,
        out_shape=pltpu.VMEM((2, kv.shape[1], 4 * CHUNK), kv.dtype),
        scratch_shapes=[pltpu.SemaphoreType.DMA((8,))],
        compiler_params=SMALL,
    )(where, lengths, kv)


def owned_chunk(plan, code):
    item, j = (code >> 3) & 1, code & 7
    at = META + item * N_META
    ident = plan[at + 2] + j
    return item, j, ident, ident < plan[at + 1]


def store_owned(plan, head, code, rows, cache, post, sem, start):
    item, j, ident, real = owned_chunk(plan, code)
    per_half = 2048 // CHUNK
    here = ident >> 3 == head

    @pl.when(real & here)
    def _():
        copy = pltpu.make_async_copy(rows, cache.at[item, :, lanes(ident & (per_half - 1))], sem)
        copy.start() if start else copy.wait()

    @pl.when(real & ~here)
    def _():
        copy = pltpu.make_async_copy(rows, post.at[item, :, lanes(j & 3)], sem)
        copy.start() if start else copy.wait()


def step_kernel(now, *refs):
    taking = now is not None
    if not taking:
        time, *refs = refs
        now = time[0]
    plan, kv, pre, *refs = refs
    if taking:
        query, query_other, *refs = refs
        arrived, refs = refs[:3], refs[8:]
        sends, inbox, (cache, post, total, stats, local, sems) = refs[:3], refs[3], refs[4:]
    else:
        arrived, refs = refs[:3], refs[4:]
        sends, (inbox, sems) = refs[:3], refs[3:]
    head = plan[HEAD]
    to_send, to_keep = plan[SEND + now], plan[KEEP + now]
    codes = [(to_send >> (8 * kind)) & 255 for kind in range(3)]
    places = [(to_keep >> (8 * kind)) & 255 for kind in range(3)]
    waiting = OWNED if taking else NOTHING

    def load_from(source, kind):
        return pltpu.make_async_copy(source, sends[kind], sems.at[kind])

    def keep(kind):
        place = jnp.minimum(places[kind], SLOTS + 15)
        return pltpu.make_async_copy(arrived[kind], inbox.at[place], sems.at[3 + kind])

    for kind in range(3):
        code = codes[kind]

        @pl.when(code < FROM_PRE)
        def _():
            load_from(kv.at[code >> 3, :, lanes(code & 7)], kind).start()

        @pl.when((code >= FROM_PRE) & (code < FROM_LINK))
        def _():
            load_from(pre.at[(code - FROM_PRE) >> 2, :, lanes(code & 3)], kind).start()

        for other in range(3):

            @pl.when(code == FROM_LINK + other)
            def _():
                load_from(arrived[other], kind).start()

        @pl.when((code >= FROM_INBOX) & (code < NOTHING))
        def _():
            load_from(inbox.at[code - FROM_INBOX], kind).start()

        @pl.when(places[kind] < waiting)
        def _():
            keep(kind).start()

    if taking:
        staying = plan[STAY + now]

        def load_local():
            item = (staying >> 3) & 1
            source = jnp.maximum(plan[META + item * N_META + 4], 0)
            return pltpu.make_async_copy(kv.at[source, :, lanes(staying & 7)], local, sems.at[6])

        @pl.when(staying >= 0)
        def _():
            load_local().start()

        def take(code, rows, sem):
            store_owned(plan, head, code, rows, cache, post, sem, True)
            item, j, _, _ = owned_chunk(plan, code)
            absorb(plan, item, j, rows, query, query_other, total, stats)

        for kind in range(3):

            @pl.when((places[kind] >= OWNED) & (places[kind] < NOTHING))
            def _():
                take(places[kind] - OWNED, arrived[kind], sems.at[3 + kind])

        @pl.when(staying >= 0)
        def _():
            load_local().wait()
            take(staying, local, sems.at[7])
            store_owned(plan, head, staying, local, cache, post, sems.at[7], False)

    for kind in range(3):

        @pl.when(codes[kind] < NOTHING)
        def _():
            load_from(arrived[kind], kind).wait()

        @pl.when(places[kind] < waiting)
        def _():
            keep(kind).wait()

        if taking:

            @pl.when((places[kind] >= OWNED) & (places[kind] < NOTHING))
            def _():
                code = places[kind] - OWNED
                store_owned(plan, head, code, arrived[kind], cache, post, sems.at[3 + kind], False)


def in_smem(plan):
    return pltpu.with_memory_space_constraint(plan, pltpu.SMEM)


def in_hbm(arrays):
    return [pltpu.with_memory_space_constraint(a, pltpu.HBM) for a in arrays]


def in_vmem(arrays):
    return [pltpu.with_memory_space_constraint(a, pltpu.VMEM) for a in arrays]


def like(state):
    shapes = [pltpu.HBM(a.shape, a.dtype) for a in state[:3]]
    return shapes + [pltpu.VMEM(a.shape, a.dtype) for a in state[3:]]


def one_step(time, plan, kv, pre, queries, arrived, state):
    taking = isinstance(time, int)
    inbox = state[0]
    times = [] if taking else [jnp.full((1,), time, jnp.int32)]
    piece = pltpu.VMEM(inbox.shape[1:], inbox.dtype)
    queries = queries if taking else ()
    state = state if taking else state[:1]
    first = len(times) + 3 + len(queries) + 3
    wide = [ANY] * 3 + [VMEM] * 2 if taking else [ANY]
    scratch = [pltpu.VMEM(inbox.shape[1:], inbox.dtype)] if taking else []
    out = pl.pallas_call(
        functools.partial(step_kernel, time if taking else None),
        in_specs=[SMEM] * (len(times) + 1) + [ANY] * 2 + [VMEM] * (len(queries) + 3) + wide,
        out_specs=[VMEM] * 3 + wide,
        out_shape=[piece] * 3 + like(state),
        input_output_aliases={first + k: 3 + k for k in range(len(state))},
        scratch_shapes=scratch + [pltpu.SemaphoreType.DMA((8,))],
        compiler_params=SMALL,
        cost_estimate=pl.CostEstimate(
            flops=0, bytes_accessed=12 * inbox.shape[1] * CHUNK, transcendentals=0
        ),
    )(
        *times, in_smem(plan), *in_hbm([kv, pre]), *in_vmem([*queries, *arrived]),
        *in_hbm(state[:3]), *in_vmem(state[3:]),
    )
    return out[:3], out[3:]


def finish_kernel(time, plan, query, query_other, inbox, *refs):
    arrived, refs = refs[: 3 * LAG], refs[3 * LAG + 4 :]
    cache, post, total, stats, others_out, local, sems = refs
    head = plan[HEAD]
    own = others_out.shape[1]

    def take_waiting(code, _):
        row = plan[LAST + code]

        @pl.when((row >= UNROLLED) & (row < time[0]))
        def _():
            load = pltpu.make_async_copy(inbox.at[OWNED + code], local, sems.at[3 * LAG])
            load.start()
            load.wait()
            store_owned(plan, head, code, local, cache, post, sems.at[3 * LAG], True)
            item, j, _, _ = owned_chunk(plan, code)
            absorb(plan, item, j, local, query, query_other, total, stats)
            store_owned(plan, head, code, local, cache, post, sems.at[3 * LAG], False)

        return 0

    @pl.when(time[0] > UNROLLED)
    def _():
        lax.fori_loop(0, 16, take_waiting, 0)

    for start in (True, False):
        for late in range(LAG):
            word = plan[KEEP + time[0] + late]
            for kind in range(3):
                place = (word >> (8 * kind)) & 255
                rows = arrived[3 * late + kind]
                code = place - OWNED

                @pl.when((place >= OWNED) & (place < NOTHING))
                def _():
                    sem = sems.at[3 * late + kind]
                    store_owned(plan, head, code, rows, cache, post, sem, start)
                    if start:
                        item, j, _, _ = owned_chunk(plan, code)
                        absorb(plan, item, j, rows, query, query_other, total, stats)

    others = pl.ds(own, own)
    for item in range(others_out.shape[0]):
        weight_sum = stats[item, 1, others, :]
        seen = weight_sum > 0
        safe = jnp.where(seen, weight_sum, 1.0)
        level = jnp.where(seen, stats[item, 0, others, :] + jnp.log(safe), big_negative)
        inverse = jnp.concatenate([1.0 / safe] * (DL // 128), axis=1)
        mean = total[item, others, :] * inverse
        others_out[item, :, pl.ds(0, DL)] = mean.astype(others_out.dtype)
        rough = level.astype(others_out.dtype)
        rest = (level - rough.astype(jnp.float32)).astype(others_out.dtype)
        lane = lax.broadcasted_iota(jnp.int32, (own, 128), 1)
        others_out[item, :, pl.ds(DL, 128)] = jnp.where(lane == 0, rough, rest)


def finish(time, plan, query, query_other, arrived, state):
    items, rows, width = state[3].shape
    shapes = like(state)[1:]
    return pl.pallas_call(
        finish_kernel,
        in_specs=[SMEM] * 2 + [VMEM] * 2 + [ANY] + [VMEM] * (3 * LAG) + [ANY] * 2 + [VMEM] * 2,
        out_specs=[ANY] * 2 + [VMEM] * 3,
        out_shape=shapes
        + [pltpu.VMEM((items, rows // 2, width + 128), jnp.bfloat16)],
        input_output_aliases={5 + 3 * LAG + k: k for k in range(4)},
        scratch_shapes=[
            pltpu.VMEM(state[0].shape[1:], state[0].dtype),
            pltpu.SemaphoreType.DMA((3 * LAG + 1,)),
        ],
        compiler_params=SMALL,
    )(
        time, in_smem(plan), *in_vmem([query, query_other]), *in_hbm(state[:1]), *in_vmem(arrived),
        *in_hbm(state[1:3]), *in_vmem(state[3:]),
    )


def end_kernel(plan, post, total, stats, others, _, out, cache, sems):
    per_half = 2048 // CHUNK

    def rows(start):
        for item in range(2):
            at = META + item * N_META
            n, stays, h = plan[at + 1], plan[at + 4], plan[at + 5]
            for q in range(4):

                @pl.when((plan[HEAD] == 0) & (stays < 0) & (h + q < jnp.minimum(n, per_half)))
                def _():
                    copy = pltpu.make_async_copy(
                        post.at[item, :, pl.ds(q * CHUNK, CHUNK)],
                        cache.at[item, :, lanes(jnp.minimum(h + q, per_half - 1))],
                        sems.at[item * 4 + q],
                    )
                    copy.start() if start else copy.wait()

    rows(True)
    items, own, _ = others.shape
    steps, _, heads, _ = out.shape
    mine = pl.ds(0, own)
    for item in range(items):
        top_one, sum_one = stats[item, 0, mine, :][:, :1], stats[item, 1, mine, :][:, :1]
        level = others[item, :, pl.ds(DL, 128)].astype(jnp.float32)
        level = level[:, :1] + level[:, 1:2]
        top = jnp.maximum(top_one, level)
        scale_one, scale_two = jnp.exp(top_one - top), jnp.exp(level - top)
        inverse = 1.0 / (sum_one * scale_one + scale_two)
        theirs = others[item, :, pl.ds(0, DL)].astype(jnp.float32)
        result = total[item, mine, :] * (scale_one * inverse) + theirs * (scale_two * inverse)
        result = result.astype(out.dtype)
        for step in range(steps):
            out[step, item] = result[step * heads : (step + 1) * heads]
    rows(False)


def end(plan, post, total, stats, others, cache, steps, heads):
    return pl.pallas_call(
        end_kernel,
        in_specs=[SMEM] + [VMEM] * 4 + [ANY],
        out_specs=[VMEM, ANY],
        out_shape=[
            jax.ShapeDtypeStruct((steps, total.shape[0], heads, DL), jnp.bfloat16),
            pltpu.HBM(cache.shape, cache.dtype),
        ],
        input_output_aliases={5: 1},
        scratch_shapes=[pltpu.SemaphoreType.DMA((8,))],
        compiler_params=SMALL,
    )(in_smem(plan), *in_vmem([post, total, stats, others]), *in_hbm([cache]))


def exchanges(zs):
    even, odd, across = [], [], []
    for z in range(zs):
        for y in range(2):
            across.append((z * 2 + y, z * 2 + 1 - y))
            if z + 1 < zs:
                pairs = even if z % 2 == 0 else odd
                pairs.append((z * 2 + y, z * 2 + 2 + y))
                pairs.append((z * 2 + 2 + y, z * 2 + y))
    return even, odd, across


def routed(zs, kv, lengths, slot_of, query, new_latent):
    kinds = exchanges(zs)
    steps, items, heads, width = query.shape
    where = jnp.stack([lax.axis_index("seq"), lax.axis_index("head")]).astype(jnp.int32)
    kv = jnp.swapaxes(kv, 1, 2)
    swap = [(0, 1), (1, 0)]
    fresh = jnp.pad(jnp.swapaxes(new_latent, 0, 1), ((0, 0), (0, 128 - steps), (0, 0)))
    pre = lax.ppermute(hand_over(where, lengths, kv), "head", [(0, 1)])
    query_other = lax.ppermute(query, "head", swap)
    plan, *state = make_plan(zs, where, lengths, slot_of, query, fresh, kv)
    plan, query_other = lax.optimization_barrier((plan, query_other))

    def run(begin, count, arrived, state):
        for k in range(count):
            queries = (query, query_other)
            sends, state = one_step(begin + k, plan, kv, pre, queries, arrived[0], state)
            new = [lax.ppermute(s, "seq", pairs) for s, pairs in zip(sends, kinds)]
            arrived = arrived[1:] + [new]
        return arrived, state

    nothing = [jnp.zeros((width, CHUNK), kv.dtype)] * 3
    arrived, state = run(0, UNROLLED, [nothing] * LAG, state)
    last_step = plan[META + 2 * N_META]

    def more(carry):
        return carry[0] < last_step

    def body(carry):
        time, arrived, inbox = carry
        arrived, (inbox,) = run(time, BODY, arrived, [inbox])
        return time + BODY, arrived, inbox

    inbox, *state = state
    time, arrived, inbox = lax.while_loop(more, body, (jnp.int32(UNROLLED), arrived, inbox))
    cache, post, total, stats, others = finish(
        time[None], plan, query, query_other, sum(arrived, []), [inbox, *state]
    )
    post = lax.ppermute(post, "head", [(1, 0)])
    others = lax.ppermute(others, "head", swap)
    attended, cache = end(plan, post, total, stats, others, cache, steps, heads)
    return attended, jnp.swapaxes(cache, 1, 2)


def merged_2(shard, axis, combine):
    everything = jax.tree.map(
        lambda part, kind: lax.all_gather(part.astype(kind), axis),
        shard,
        (jnp.bfloat16, jnp.bfloat16, jnp.bfloat16),
    )

    def take(k):
        return jax.tree.map(lambda part, own: part[k].astype(own.dtype), everything, shard)

    return lax.fori_loop(
        1, lax.axis_size(axis), lambda k, so_far: combine(so_far, take(k)), take(0)
    )


def join_partials(first, second):
    top = jnp.maximum(first[0], second[0])
    scale_one = jnp.exp(first[0] - top)
    scale_two = jnp.exp(second[0] - top)
    total = first[1] * scale_one + second[1] * scale_two
    summed = first[2] * scale_one[..., None] + second[2] * scale_two[..., None]
    return (top, total, summed)


def balanced(kv, lengths, slot_of, query, new_latent):
    req = kv.shape[0]
    half = kv.shape[1]
    count = lengths.shape[0]
    steps_new = query.shape[0]
    heads_here = query.shape[2]
    pieces = lax.all_to_all(kv, "seq", split_axis=1, concat_axis=0, tiled=True)
    inverse = jnp.zeros((count,), jnp.int32).at[slot_of].set(jnp.arange(count, dtype=jnp.int32))
    ordered = jnp.take(pieces, inverse, axis=0)
    cache = lax.all_to_all(ordered, "seq", split_axis=0, concat_axis=1, tiled=True)
    my_lens = lax.dynamic_slice_in_dim(
        jnp.take(lengths, inverse, axis=0), lax.axis_index("seq") * req, req
    )
    head_pos = lax.axis_index("head")
    rows = steps_new * heads_here
    row_step = jnp.arange(rows, dtype=jnp.int32) // heads_here
    valid_two = jnp.arange(steps_new, dtype=jnp.int32)[None, :] <= row_step[:, None]
    results = []
    every_query = lax.all_gather(query, "head", axis=2, tiled=True)
    heads_all = every_query.shape[2]
    rows_all = steps_new * heads_all
    positions = head_pos * half + jnp.arange(half, dtype=jnp.int32)
    tops = []
    totals = []
    sums = []
    for item in range(req):
        queries = every_query[:, item].reshape(rows_all, every_query.shape[3])
        valid_one = positions[None, :] < my_lens[item]
        cache_scores = (
            jnp.einsum("nd,td->nt", queries, cache[item], preferred_element_type=jnp.float32)
            * score_scale
        )
        top = jnp.max(jnp.where(valid_one, cache_scores, big_negative), axis=1)
        weight_one = jnp.where(valid_one, jnp.exp(cache_scores - top[:, None]), 0.0)
        tops.append(top)
        totals.append(jnp.sum(weight_one, axis=1))
        sums.append(
            jnp.dot(
                weight_one.astype(jnp.bfloat16),
                cache[item][:, :DL],
                preferred_element_type=jnp.float32,
            )
        )
    merged = merged_2((jnp.stack(tops), jnp.stack(totals), jnp.stack(sums)), "head", join_partials)
    start = head_pos * heads_here
    own_top = lax.dynamic_slice_in_dim(
        merged[0].reshape(req, steps_new, heads_all), start, heads_here, 2
    ).reshape(req, rows)
    own_total = lax.dynamic_slice_in_dim(
        merged[1].reshape(req, steps_new, heads_all), start, heads_here, 2
    ).reshape(req, rows)
    own_sum = lax.dynamic_slice_in_dim(
        merged[2].reshape(req, steps_new, heads_all, DL), start, heads_here, 2
    ).reshape(req, rows, DL)
    for item in range(req):
        queries = query[:, item].reshape(rows, query.shape[3])
        fresh = new_latent[:, item]
        new_scores = (
            jnp.einsum("nd,td->nt", queries, fresh, preferred_element_type=jnp.float32)
            * score_scale
        )
        top = jnp.maximum(
            own_top[item], jnp.max(jnp.where(valid_two, new_scores, big_negative), axis=1)
        )
        rescale = jnp.exp(own_top[item] - top)
        weight_two = jnp.where(valid_two, jnp.exp(new_scores - top[:, None]), 0.0)
        total = own_total[item] * rescale + jnp.sum(weight_two, axis=1)
        summed = own_sum[item] * rescale[:, None]
        summed = summed + jnp.dot(
            weight_two.astype(jnp.bfloat16), fresh[:, :DL], preferred_element_type=jnp.float32
        )
        results.append(
            (summed / total[:, None]).astype(jnp.bfloat16).reshape(steps_new, heads_here, DL)
        )
    return (jnp.stack(results, axis=1), cache)


def solution(mesh):
    local = functools.partial(routed, 4) if mesh.shape["seq"] == 8 else balanced
    return jax.shard_map(
        local,
        mesh=mesh,
        in_specs=(
            P(("groups", "seq"), "head", None),
            P("groups"),
            P("groups"),
            P(None, ("groups", "seq"), "head", None),
            P(None, ("groups", "seq"), None),
        ),
        out_specs=(P(None, ("groups", "seq"), "head", None), P(("groups", "seq"), "head", None)),
        check_vma=False,
    )
```
